32 devices in a mesh: gx: 8 (over y, x, core), gy: 4 (over z).
Axes of the slice: x: 2, y: 2, z: 4, core: 2. Of those that a mesh axis runs over, the one named last changes fastest.
Arguments:
- right_side: float32 [32, 32, 512], P('gx', 'gy'), may hold values from -18 to 18
- labels: int32 [32, 32, 512], P('gx', 'gy'), may hold values from 0 to 2
- conduct_table: float32 [3], replicated, may hold values from 0.2 to 5
Outputs:
- correction: float32 [32, 32, 512], P('gx', 'gy')
The draws below stay inside these ranges and needn't reach their ends.
All inputs are finite; a program needn't handle non-finite values.
Results may differ from the reference program's by a relative error of at most 0.0003.
Values sent between devices are 32-bit elements; how exact they have to be, the bound alone decides.
A program may use at most 128 MiB of HBM per device.

```python
import math
import jax
import jax.numpy as jnp

NZ = 512
SWEEPS = 8
NX = 32
NY = 32


def draw_right_side(key, part):
    shape = (NX, NY, NZ)
    return jnp.clip(3.0 * jax.random.normal(key, shape, jnp.float32), -18.0, 18.0)


def set_ends(result, own_key, smallest, top_value):
    longest = result.shape.index(max(result.shape))
    spots = []
    for shift in (0, 1):
        where = [jax.random.randint(jax.random.fold_in(own_key, axis), (), 0, length) for axis, length in enumerate(result.shape)]
        where[longest] = (where[longest] + shift) % result.shape[longest]
        spots.append(tuple(where))
    return result.at[spots[0]].set(smallest).at[spots[1]].set(top_value)


def setup_inputs(seed: int = 0) -> dict:
    key_of = jax.random.split(jax.random.key(seed), 4)
    right_side = draw_right_side(jax.random.fold_in(key_of[3], 71), 0)
    labels = set_ends(jax.random.randint(key_of[1], (NX, NY, NZ), 0, 3), jax.random.fold_in(key_of[1], 1), 0, 2).astype(jnp.int32)
    conduct_table = jnp.clip(jnp.exp(jax.random.uniform(key_of[2], (3,), jnp.float32, math.log(0.2), math.log(5.0))), 0.2, 5.0)
    return {"right_side": right_side, "labels": labels, "conduct_table": conduct_table}


OMEGA = 0.8


def lookup(labels, table):
    return jnp.where(labels == 0, table[0], jnp.where(labels == 1, table[1], table[2]))


def face_couplings(padded):
    own = padded[1:-1, 1:-1, 1:-1]
    own = jnp.where(own > 0.0, own, 1.0)

    def across(beside):
        beside = jnp.where(beside > 0.0, beside, own)
        return 2.0 * (own * beside) / (own + beside)

    return jnp.stack([across(padded[:-2, 1:-1, 1:-1]), across(padded[2:, 1:-1, 1:-1]),
                      across(padded[1:-1, :-2, 1:-1]), across(padded[1:-1, 2:, 1:-1]),
                      across(padded[1:-1, 1:-1, :-2]), across(padded[1:-1, 1:-1, 2:])])


def coupled(couplings, padded):
    total = couplings[0] * padded[:-2, 1:-1, 1:-1] + couplings[1] * padded[2:, 1:-1, 1:-1]
    total = total + couplings[2] * padded[1:-1, :-2, 1:-1] + couplings[3] * padded[1:-1, 2:, 1:-1]
    total = total + couplings[4] * padded[1:-1, 1:-1, :-2] + couplings[5] * padded[1:-1, 1:-1, 2:]
    return total


def relax(couplings, diagonal, source, field, padded):
    image = diagonal * field - coupled(couplings, padded)
    return field + OMEGA * (source - image) / diagonal


def residual_of(couplings, diagonal, source, field, padded):
    return source - (diagonal * field - coupled(couplings, padded))


def coarsen_couplings(couplings):
    extent = couplings.shape
    blocks = couplings.reshape(6, extent[1] // 2, 2, extent[2] // 2, 2, extent[3] // 2, 2)
    lower_one = jnp.sum(blocks[0][:, 0], axis=(2, 4))
    upper_one = jnp.sum(blocks[1][:, 1], axis=(2, 4))
    lower_two = jnp.sum(blocks[2][:, :, :, 0], axis=(1, 4))
    upper_two = jnp.sum(blocks[3][:, :, :, 1], axis=(1, 4))
    lower_three = jnp.sum(blocks[4][..., 0], axis=(1, 3))
    upper_three = jnp.sum(blocks[5][..., 1], axis=(1, 3))
    return jnp.stack([lower_one, upper_one, lower_two, upper_two, lower_three, upper_three])


def restrict(field):
    extent = field.shape
    return jnp.sum(field.reshape(extent[0] // 2, 2, extent[1] // 2, 2, extent[2] // 2, 2), axis=(1, 3, 5))


def prolong(field):
    extent = field.shape
    spread = jnp.broadcast_to(field[:, None, :, None, :, None], (extent[0], 2, extent[1], 2, extent[2], 2))
    return spread.reshape(2 * extent[0], 2 * extent[1], 2 * extent[2])


def smooth(couplings, diagonal, source, field, count):
    for repeat in range(count):
        field = relax(couplings, diagonal, source, field, jnp.pad(field, 1))
    return field


def reference(right_side, labels, conduct_table):
    conduct = lookup(labels, conduct_table)
    fine_couplings = face_couplings(jnp.pad(conduct, 1))
    fine_diagonal = jnp.sum(fine_couplings, axis=0)
    fine_iterate = smooth(fine_couplings, fine_diagonal, right_side, jnp.zeros_like(right_side), 2)
    fine_residual = residual_of(fine_couplings, fine_diagonal, right_side, fine_iterate, jnp.pad(fine_iterate, 1))
    middle_source = restrict(fine_residual)
    middle_couplings = coarsen_couplings(fine_couplings)
    middle_diagonal = jnp.sum(middle_couplings, axis=0)
    middle_iterate = smooth(middle_couplings, middle_diagonal, middle_source, jnp.zeros_like(middle_source), 2)
    middle_residual = residual_of(middle_couplings, middle_diagonal, middle_source, middle_iterate, jnp.pad(middle_iterate, 1))
    coarse_source = restrict(middle_residual)
    coarse_couplings = coarsen_couplings(middle_couplings)
    coarse_diagonal = jnp.sum(coarse_couplings, axis=0)
    coarse_iterate = smooth(coarse_couplings, coarse_diagonal, coarse_source, jnp.zeros_like(coarse_source), SWEEPS)
    middle_iterate = middle_iterate + prolong(coarse_iterate)
    middle_iterate = smooth(middle_couplings, middle_diagonal, middle_source, middle_iterate, 1)
    fine_iterate = fine_iterate + prolong(middle_iterate)
    return smooth(fine_couplings, fine_diagonal, right_side, fine_iterate, 1)
```

```python
import functools

import jax
import jax.numpy as jnp
from jax import lax
from jax.experimental import pallas as pl
from jax.experimental.pallas import tpu as pltpu
from jax.sharding import PartitionSpec as P

SWEEPS = 8
OMEGA = 0.8
KEEP = 1.0 - OMEGA
MESH = pl.DeviceIdType.MESH
TINY = 1e-30

DIRECTIONS = ((1, 0), (-1, 0), (0, 1), (0, -1), (1, 1), (1, -1), (-1, 1), (-1, -1))

ROW0 = 4


def span(step, width, count, first):
    if step == 0:
        return first, first, count
    if step > 0:
        return first + count - width, first - width, width
    return first, first + count, width


def shift(v, by, axis):
    return pltpu.roll(v, by % v.shape[axis], axis)


def flow(low, high, hy, hz, v_low, v, v_high, s):
    a, b = v.ndim - 2, v.ndim - 1
    total = low * v_low + high * v_high
    total = total + hy * shift(v, -s, a) + shift(hy * v, s, a)
    return total + hz * shift(v, -s, b) + shift(hz * v, s, b)


def exact_dot(a, b):
    return jnp.dot(a, b, preferred_element_type=jnp.float32, precision=lax.Precision.HIGHEST)


def kernel(gx, gy, nx, ny, rhs_ref, lab_ref, tab_ref, out_ref, K, R, V1, V2, CC, CB, CR, own_cc, own_cb,
           bytes_cc, bytes_cb, send, recv, g_send, g_recv):
    i = lax.axis_index("gx")
    j = lax.axis_index("gy")
    n = gx * gy
    me = i * gy + j
    nz = rhs_ref.shape[2]
    mx = nx // 2
    tile = (2 * ROW0 + ny, nz)

    for buf in (K, R, V1, V2):
        buf[...] = jnp.zeros(buf.shape, jnp.float32)

    def other(k):
        t = lax.rem(me + k, n)
        return (t // gy, lax.rem(t, gy))

    barrier = pltpu.get_barrier_semaphore()

    def greet(k, c):
        pl.semaphore_signal(barrier, inc=1, device_id=other(k), device_id_type=MESH)
        return c

    lax.fori_loop(1, n, greet, 0)
    rows = slice(ROW0, ROW0 + ny)
    t0, t1, t2 = tab_ref[0], tab_ref[1], tab_ref[2]
    labels = lab_ref[...]
    K[3:3 + nx, rows, :] = jnp.where(labels == 0, t0, jnp.where(labels == 1, t1, t2))
    R[2:2 + nx, rows, :] = rhs_ref[...]
    pl.semaphore_wait(barrier, n - 1)

    def there(dx, dy):
        ok = None
        for at, d, size in ((i, dx, gx), (j, dy, gy)):
            if d:
                c = (at < size - 1) if d > 0 else (at > 0)
                ok = c if ok is None else jnp.logical_and(ok, c)
        return ok

    def halo_copy(buf, which, d, x0, cx, y0, cy, wx, wy, corner_x, corner_y):
        dx, dy = DIRECTIONS[d]
        both = dx != 0 and dy != 0
        sx, tx, lx = span(dx, corner_x if both else wx, cx, x0)
        sy, ty, ly = span(dy, corner_y if both else wy, cy, y0)
        return pltpu.make_async_remote_copy(
            src_ref=buf.at[sx:sx + lx, sy:sy + ly, :],
            dst_ref=buf.at[tx:tx + lx, ty:ty + ly, :],
            send_sem=send.at[which, d],
            recv_sem=recv.at[which, d],
            device_id=(i + dx, j + dy),
            device_id_type=MESH,
        )

    halos = {
        0: (K, 3, nx, ROW0, ny, 3, 3, 2, 2),
        1: (R, 2, nx, ROW0, ny, 2, 2, 1, 1),
        2: (V1, 2, mx, ROW0, ny, 2, 4, 1, 2),
        3: (V2, 2, mx, ROW0, ny, 2, 4, 1, 2),
    }

    def each(which, what):
        for d, (dx, dy) in enumerate(DIRECTIONS):
            sign = -1 if what == "wait_recv" else 1

            @pl.when(there(sign * dx, sign * dy))
            def _():
                buf, *sizes = halos[which]
                getattr(halo_copy(buf, which, d, *sizes), what)()

    each(0, "start")
    each(1, "start")

    row = lax.broadcasted_iota(jnp.int32, tile, 0)
    lane = lax.broadcasted_iota(jnp.int32, tile, 1)
    odd_row = (row & 1) == 1
    odd_lane = (lane & 1) == 1
    last_lane = lane == nz - 1
    first_lane = lane == 0

    def pair(v, axis):
        odd = odd_row if axis == 0 else odd_lane
        return v + jnp.where(odd, shift(v, 1, axis), shift(v, -1, axis))

    def upper(v, axis):
        odd = odd_row if axis == 0 else odd_lane
        return jnp.where(odd, v, shift(v, -1, axis))

    each(0, "wait_recv")
    nk = nx + 6
    k = [K[x] for x in range(nk)]

    def harmonic(a, b):
        return 2.0 * (a * b) / jnp.maximum(a + b, TINY)

    hx = [harmonic(k[x], k[x + 1]) for x in range(nk - 1)]
    hy, hz, edge, diag, inv = ([None] * nk for _ in range(5))
    for x in range(1, nk - 1):
        a = k[x]
        y_up, y_low = shift(a, -1, 0), shift(a, 1, 0)
        z_up = jnp.where(last_lane, 0.0, shift(a, -1, 1))
        hy[x] = harmonic(a, y_up)
        hz[x] = harmonic(a, z_up)
        beyond = jnp.where(k[x - 1] > 0.0, 0.0, a) + jnp.where(k[x + 1] > 0.0, 0.0, a)
        beyond = beyond + jnp.where(y_up > 0.0, 0.0, a) + jnp.where(y_low > 0.0, 0.0, a)
        edge[x] = beyond + jnp.where(first_lane, a, 0.0) + jnp.where(last_lane, a, 0.0)
        diag[x] = (hx[x - 1] + hx[x]) + (hy[x] + shift(hy[x], 1, 0)) + (hz[x] + shift(hz[x], 1, 1)) + edge[x]
        inv[x] = OMEGA / jnp.maximum(diag[x], TINY)

    nm = mx + 4
    gxu = [None] * nm
    gyu, gzu, medge, mdiag, minv = ([None] * nm for _ in range(5))
    for m in range(nm - 1):
        gxu[m] = pair(pair(hx[2 * m], 0), 1)
    for m in range(1, nm - 1):
        x = 2 * m - 1
        gyu[m] = upper(pair(hy[x] + hy[x + 1], 1), 0)
        gzu[m] = upper(pair(hz[x] + hz[x + 1], 0), 1)
        medge[m] = pair(pair(edge[x] + edge[x + 1], 0), 1)
        mdiag[m] = (gxu[m - 1] + gxu[m]) + (gyu[m] + shift(gyu[m], 2, 0))
        mdiag[m] = mdiag[m] + (gzu[m] + shift(gzu[m], 2, 1)) + medge[m]
        minv[m] = OMEGA / jnp.maximum(mdiag[m], TINY)

    each(1, "wait_recv")
    u1, u2 = [None] * nk, [None] * nk
    for x in range(1, nk - 1):
        u1[x] = R[x - 1] * inv[x]
    for x in range(2, nk - 2):
        around = flow(hx[x - 1], hx[x], hy[x], hz[x], u1[x - 1], u1[x], u1[x + 1], 1)
        u2[x] = (1.0 + KEEP) * u1[x] + inv[x] * around
    res = [None] * nk
    for x in range(3, nk - 3):
        around = flow(hx[x - 1], hx[x], hy[x], hz[x], u2[x - 1], u2[x], u2[x + 1], 1)
        res[x] = diag[x] * (u1[x] * (1.0 / OMEGA) - u2[x]) + around

    for m in range(2, nm - 2):
        x = 2 * m - 1
        source = pair(pair(res[x] + res[x + 1], 0), 1)
        V1[m, rows, :] = (source * minv[m])[rows]
    each(2, "start")

    def cells(v):
        return jnp.concatenate([v[0:1] + v[2:3], v[4:5] + v[6:7]], axis=0)

    z = lax.broadcasted_iota(jnp.int32, (nz, nz // 4), 0)
    q = lax.broadcasted_iota(jnp.int32, (nz, nz // 4), 1)
    same = (z // 4) == q
    both = jnp.where(same & ((z & 1) == 0), 1.0, 0.0)
    top = jnp.where(same & ((z & 3) == 3), 1.0, 0.0)
    m = 2
    ux = exact_dot(gxu[m + 1][rows], both)
    uy = exact_dot((gyu[m] + gyu[m + 1])[rows], both)
    uz = exact_dot((gzu[m] + gzu[m + 1])[rows], top)
    ue = exact_dot((medge[m] + medge[m + 1])[rows], both)
    own_cc[0] = cells(ux)
    own_cc[1] = jnp.concatenate([uy[2:3], uy[6:7]], axis=0)
    own_cc[2] = cells(uz)
    own_cc[3] = cells(ue)

    spot_cc = CC.at[:, i, pl.ds(2 * j, 2), :]
    spot_cb = CB.at[i, pl.ds(2 * j, 2), :]

    def spread(src, dst, which):
        def one(t, c):
            pltpu.make_async_remote_copy(
                src_ref=src, dst_ref=dst, send_sem=g_send.at[which], recv_sem=g_recv.at[which],
                device_id=other(t), device_id_type=MESH,
            ).start()
            return c

        lax.fori_loop(1, n, one, 0)
        pltpu.make_async_copy(src, dst, g_recv.at[which]).start()

    spread(own_cc, spot_cc, 0)

    each(2, "wait_recv")
    v1 = [V1[m] for m in range(nm)]
    v2 = [None] * nm
    for m in range(1, nm - 1):
        around = flow(gxu[m - 1], gxu[m], gyu[m], gzu[m], v1[m - 1], v1[m], v1[m + 1], 2)
        v2[m] = (1.0 + KEEP) * v1[m] + minv[m] * around
    for m in range(2, nm - 2):
        V2[m, rows, :] = v2[m][rows]
    total = None
    for m in range(2, nm - 2):
        around = flow(gxu[m - 1], gxu[m], gyu[m], gzu[m], v2[m - 1], v2[m], v2[m + 1], 2)
        r = mdiag[m] * (v1[m] * (1.0 / OMEGA) - v2[m]) + around
        total = r if total is None else total + r
    own_cb[...] = cells(exact_dot(total[rows], both))
    spread(own_cb, spot_cb, 1)
    each(3, "start")

    pltpu.make_async_copy(CC, CC, g_recv.at[0]).wait()
    cx, cy, cz, ce = CC[0], CC[1], CC[2], CC[3]

    def before(v):
        return jnp.concatenate([v[-1:], v[:-1]], axis=0)

    def after(v):
        return jnp.concatenate([v[1:], v[:1]], axis=0)

    cxl = before(cx)
    cdiag = (cx + cxl) + (cy + shift(cy, 1, 1)) + (cz + shift(cz, 1, 2)) + ce
    cinv = OMEGA / cdiag
    cyl, czl = shift(cy, 1, 1) * cinv, shift(cz, 1, 2) * cinv
    cx, cxl, cy, cz = cx * cinv, cxl * cinv, cy * cinv, cz * cinv
    pltpu.make_async_copy(CB, CB, g_recv.at[1]).wait()
    b = CB[...] * cinv
    v = b
    for step in range(SWEEPS - 1):
        around = cxl * before(v) + cx * after(v)
        around = around + cyl * shift(v, 1, 1) + cy * shift(v, -1, 1)
        around = around + czl * shift(v, 1, 2) + cz * shift(v, -1, 2)
        v = KEEP * v + b + around
    zero = jnp.zeros((1,) + v.shape[1:], jnp.float32)
    CR[0:1] = zero
    CR[gx + 1:gx + 2] = zero
    CR[1:gx + 1] = v

    crow = CR.shape[1]
    er = lax.broadcasted_iota(jnp.int32, (tile[0], crow), 0)
    ec = lax.broadcasted_iota(jnp.int32, (tile[0], crow), 1)
    pick = jnp.where(ec == 2 * j - 1 + er // 4, 1.0, 0.0)
    near = jnp.concatenate([exact_dot(pick, CR[i + p]) for p in range(3)], axis=0)
    zq = lax.broadcasted_iota(jnp.int32, (nz // 4, nz), 0)
    zz = lax.broadcasted_iota(jnp.int32, (nz // 4, nz), 1)
    near = exact_dot(near, jnp.where(zz // 4 == zq, 1.0, 0.0))
    near = near.reshape(3, *tile)
    each(3, "wait_recv")
    w = [V2[m] + near[m // 2] for m in range(nm)]
    v3 = [None] * nm
    for m in range(1, nm - 1):
        around = flow(gxu[m - 1], gxu[m], gyu[m], gzu[m], w[m - 1], w[m], w[m + 1], 2)
        v3[m] = KEEP * w[m] + v1[m] + minv[m] * around
    f = [None] * nk
    for x in range(2, nk - 2):
        f[x] = u2[x] + v3[(x + 1) // 2]
    for x in range(3, nk - 3):
        around = flow(hx[x - 1], hx[x], hy[x], hz[x], f[x - 1], f[x], f[x + 1], 1)
        out_ref[x - 3] = (KEEP * f[x] + u1[x] + inv[x] * around)[rows]

    for which in range(4):
        each(which, "wait_send")
    pltpu.make_async_copy(bytes_cc, bytes_cc, g_send.at[0]).wait()
    pltpu.make_async_copy(bytes_cb, bytes_cb, g_send.at[1]).wait()


def shards(gx, gy, right_side, labels, conduct_table):
    nx, ny, nz = right_side.shape
    n = gx * gy
    deep = 2 * ROW0 + ny
    cy, cz = gy * (ny // 4), nz // 4
    f32 = jnp.float32
    return pl.pallas_call(
        functools.partial(kernel, gx, gy, nx, ny),
        out_shape=jax.ShapeDtypeStruct(right_side.shape, f32),
        in_specs=[
            pl.BlockSpec(memory_space=pltpu.VMEM),
            pl.BlockSpec(memory_space=pltpu.VMEM),
            pl.BlockSpec(memory_space=pltpu.SMEM),
        ],
        out_specs=pl.BlockSpec(memory_space=pltpu.VMEM),
        scratch_shapes=[
            pltpu.VMEM((nx + 6, deep, nz), f32),
            pltpu.VMEM((nx + 4, deep, nz), f32),
            pltpu.VMEM((nx // 2 + 4, deep, nz), f32),
            pltpu.VMEM((nx // 2 + 4, deep, nz), f32),
            pltpu.VMEM((4, gx, cy, cz), f32),
            pltpu.VMEM((gx, cy, cz), f32),
            pltpu.VMEM((gx + 2, cy, cz), f32),
            pltpu.VMEM((4, 2, cz), f32),
            pltpu.VMEM((2, cz), f32),
            pltpu.VMEM((n - 1, 8, cz), f32),
            pltpu.VMEM((n - 1, 2, cz), f32),
            pltpu.SemaphoreType.DMA((4, 8)),
            pltpu.SemaphoreType.DMA((4, 8)),
            pltpu.SemaphoreType.DMA((2,)),
            pltpu.SemaphoreType.DMA((2,)),
        ],
        compiler_params=pltpu.CompilerParams(
            collective_id=0, has_side_effects=True, vmem_limit_bytes=48 * 1024 * 1024
        ),
    )(right_side, labels, conduct_table)


def solution(mesh):
    in_specs = (P("gx", "gy", None), P("gx", "gy", None), P())
    return jax.shard_map(
        functools.partial(shards, mesh.shape["gx"], mesh.shape["gy"]),
        mesh=mesh,
        in_specs=in_specs,
        out_specs=P("gx", "gy", None),
        check_vma=False,
    )
```

```python
import functools

import jax
import jax.numpy as jnp
from jax import lax
from jax.experimental import pallas as pl
from jax.experimental.pallas import tpu as pltpu
from jax.sharding import PartitionSpec as P

SWEEPS = 8
OMEGA = 0.8
KEEP = 1.0 - OMEGA
MESH = pl.DeviceIdType.MESH
TINY = 1e-30

DIRECTIONS = ((1, 0), (-1, 0), (0, 1), (0, -1), (1, 1), (1, -1), (-1, 1), (-1, -1))

ROW0 = 4


def span(step, width, count, first):
    if step == 0:
        return first, first, count
    if step > 0:
        return first + count - width, first - width, width
    return first, first + count, width


def shift(v, by, axis):
    return pltpu.roll(v, by % v.shape[axis], axis)


def flow(low, high, hy, hz, v_low, v, v_high, s):
    a, b = v.ndim - 2, v.ndim - 1
    total = low * v_low + high * v_high
    total = total + hy * shift(v, -s, a) + shift(hy * v, s, a)
    return total + hz * shift(v, -s, b) + shift(hz * v, s, b)


def turn(v, by, axis):
    tile = 8 if axis == 0 else 128
    parts = [lax.slice_in_dim(v, p, p + tile, axis=axis) for p in range(0, v.shape[axis], tile)]
    return jnp.concatenate([pltpu.roll(p, by % tile, axis) for p in parts], axis=axis)


def inverse(d):
    r = pl.reciprocal(d, approx=True)
    return r * (2.0 - d * r)


def harmonic(a, b):
    return (2.0 * (a * b)) * inverse(a + b)


def exact_dot(a, ones):
    rounded = lambda x: x.astype(jnp.bfloat16).astype(jnp.float32)
    head = rounded(a)
    rest = a - head
    middle = rounded(rest)
    parts = jnp.concatenate([head, middle, rest - middle], axis=0).astype(jnp.bfloat16)
    out = jnp.dot(parts, ones, preferred_element_type=jnp.float32)
    n = a.shape[0]
    return out[:n] + out[n:2 * n] + out[2 * n:]


def kernel(gx, gy, nx, ny, rhs_hbm, lab_hbm, tab_hbm, out_ref, K, R, V1, V2, CC, CB, CR, own_cc, own_cb,
           bytes_cc, bytes_cb, lab_ref, tab_ref, to_cell, to_lane, send, recv, g_send, g_recv, fetch):
    i = lax.axis_index("gx")
    j = lax.axis_index("gy")
    n = gx * gy
    me = i * gy + j
    nz = lab_ref.shape[2]
    mx = nx // 2
    tile = (2 * ROW0 + ny, nz)
    rows = slice(ROW0, ROW0 + ny)

    get_lab = pltpu.make_async_copy(lab_hbm, lab_ref, fetch.at[0])
    get_tab = pltpu.make_async_copy(tab_hbm, tab_ref, fetch.at[1])
    get_rhs = pltpu.make_async_copy(rhs_hbm, R.at[2:2 + nx, rows, :], fetch.at[2])
    get_lab.start()
    get_tab.start()

    K[...] = jnp.full(K.shape, TINY, jnp.float32)
    for buf in (R, V1, V2):
        buf[...] = jnp.zeros(buf.shape, jnp.float32)

    def for_others(what):
        if n <= 64:
            ti = [i] + [lax.rem(i + a, gx) for a in range(1, gx)]
            tj = [j] + [lax.rem(j + b, gy) for b in range(1, gy)]
            for b in reversed(range(gy)):
                for a in range(gx):
                    if a or b:
                        what((ti[a], tj[b]))
        else:
            def one(k, c):
                t = lax.rem(me + k, n)
                what((lax.div(t, gy), lax.rem(t, gy)))
                return c

            lax.fori_loop(1, n, one, 0)

    barrier = pltpu.get_barrier_semaphore()
    for_others(lambda dev: pl.semaphore_signal(barrier, inc=1, device_id=dev, device_id_type=MESH))
    get_rhs.start()

    z = lax.broadcasted_iota(jnp.int32, (nz, nz // 4), 0)
    q = lax.broadcasted_iota(jnp.int32, (nz, nz // 4), 1)
    to_cell[...] = jnp.where(((z >> 2) == q) & ((z & 1) == 0), 1.0, 0.0).astype(jnp.bfloat16)
    q = lax.broadcasted_iota(jnp.int32, (nz // 4, nz), 0)
    z = lax.broadcasted_iota(jnp.int32, (nz // 4, nz), 1)
    to_lane[...] = jnp.where((z >> 2) == q, 1.0, 0.0).astype(jnp.bfloat16)
    CR[...] = jnp.zeros(CR.shape, jnp.float32)

    get_lab.wait()
    get_tab.wait()
    t0, t1, t2 = tab_ref[0], tab_ref[1], tab_ref[2]
    labels = lab_ref[...]
    K[3:3 + nx, rows, :] = jnp.where(labels == 0, t0, jnp.where(labels == 1, t1, t2))
    get_rhs.wait()
    pl.semaphore_wait(barrier, n - 1)

    def there(dx, dy):
        ok = None
        for at, d, size in ((i, dx, gx), (j, dy, gy)):
            if d:
                c = (at < size - 1) if d > 0 else (at > 0)
                ok = c if ok is None else jnp.logical_and(ok, c)
        return ok

    def halo_copy(buf, which, d, x0, cx, y0, cy, wx, wy, corner_x, corner_y):
        dx, dy = DIRECTIONS[d]
        both = dx != 0 and dy != 0
        sx, tx, lx = span(dx, corner_x if both else wx, cx, x0)
        sy, ty, ly = span(dy, corner_y if both else wy, cy, y0)
        return pltpu.make_async_remote_copy(
            src_ref=buf.at[sx:sx + lx, sy:sy + ly, :],
            dst_ref=buf.at[tx:tx + lx, ty:ty + ly, :],
            send_sem=send.at[which, d],
            recv_sem=recv.at[which, d],
            device_id=(i + dx, j + dy),
            device_id_type=MESH,
        )

    halos = {
        0: (K, 3, nx, ROW0, ny, 3, 3, 2, 2),
        1: (R, 2, nx, ROW0, ny, 2, 2, 1, 1),
        2: (V1, 2, mx, ROW0, ny, 2, 4, 1, 2),
        3: (V2, 2, mx, ROW0, ny, 2, 4, 1, 2),
    }

    def each(which, what):
        for d, (dx, dy) in enumerate(DIRECTIONS):
            sign = -1 if what == "wait_recv" else 1

            @pl.when(there(sign * dx, sign * dy))
            def _():
                buf, *sizes = halos[which]
                getattr(halo_copy(buf, which, d, *sizes), what)()

    each(0, "start")
    each(1, "start")

    row = lax.broadcasted_iota(jnp.int32, tile, 0)
    lane = lax.broadcasted_iota(jnp.int32, tile, 1)
    odd_row = (row & 1) == 1
    odd_lane = (lane & 1) == 1
    last_lane = lane == nz - 1
    first_lane = lane == 0

    def pair(v, axis):
        odd = odd_row if axis == 0 else odd_lane
        return v + jnp.where(odd, turn(v, 1, axis), turn(v, -1, axis))

    def upper(v, axis):
        odd = odd_row if axis == 0 else odd_lane
        return jnp.where(odd, v, turn(v, -1, axis))

    one = lambda c: jnp.where(c, 1.0, 0.0)
    faces = one(first_lane) + one(last_lane)
    faces = faces + one((row == ROW0) & (j == 0)) + one((row == ROW0 + ny - 1) & (j == gy - 1))
    x_faces = {3: one(i == 0), 2 + nx: one(i == gx - 1)}

    each(0, "wait_recv")
    nk = nx + 6
    k = [K[x] for x in range(nk)]

    hx = [harmonic(k[x], k[x + 1]) for x in range(nk - 1)]
    hy, hz, edge, diag, inv = ([None] * nk for _ in range(5))
    for x in range(1, nk - 1):
        a = k[x]
        hy[x] = harmonic(a, shift(a, -1, 0))
        hz[x] = harmonic(a, jnp.where(last_lane, 0.0, shift(a, -1, 1)))
        edge[x] = a * ((faces + x_faces[x]) if x in x_faces else faces)
        diag[x] = (hx[x - 1] + hx[x]) + (hy[x] + shift(hy[x], 1, 0)) + (hz[x] + shift(hz[x], 1, 1)) + edge[x]
        inv[x] = OMEGA * inverse(jnp.maximum(diag[x], TINY))

    nm = mx + 4
    gxu = [None] * nm
    gyu, gzu, medge, mdiag, minv = ([None] * nm for _ in range(5))
    for m in range(nm - 1):
        gxu[m] = pair(pair(hx[2 * m], 0), 1)
    for m in range(1, nm - 1):
        x = 2 * m - 1
        gyu[m] = upper(pair(hy[x] + hy[x + 1], 1), 0)
        gzu[m] = upper(pair(hz[x] + hz[x + 1], 0), 1)
        medge[m] = pair(pair(edge[x] + edge[x + 1], 0), 1)
        mdiag[m] = (gxu[m - 1] + gxu[m]) + (gyu[m] + shift(gyu[m], 2, 0))
        mdiag[m] = mdiag[m] + (gzu[m] + shift(gzu[m], 2, 1)) + medge[m]
        minv[m] = OMEGA * inverse(jnp.maximum(mdiag[m], TINY))

    each(1, "wait_recv")
    u1, u2 = [None] * nk, [None] * nk
    for x in range(1, nk - 1):
        u1[x] = R[x - 1] * inv[x]
    for x in range(2, nk - 2):
        around = flow(hx[x - 1], hx[x], hy[x], hz[x], u1[x - 1], u1[x], u1[x + 1], 1)
        u2[x] = (1.0 + KEEP) * u1[x] + inv[x] * around
    res = [None] * nk
    for x in range(3, nk - 3):
        around = flow(hx[x - 1], hx[x], hy[x], hz[x], u2[x - 1], u2[x], u2[x + 1], 1)
        res[x] = diag[x] * (u1[x] * (1.0 / OMEGA) - u2[x]) + around

    for m in range(2, nm - 2):
        x = 2 * m - 1
        source = pair(pair(res[x] + res[x + 1], 0), 1)
        V1[m, rows, :] = (source * minv[m])[rows]
    each(2, "start")

    def cells(v):
        return jnp.concatenate([v[0:1] + v[2:3], v[4:5] + v[6:7]], axis=0)

    m = 2
    uz = jnp.where((lane & 2) == 2, gzu[m] + gzu[m + 1], 0.0)
    parts = (gxu[m + 1], gyu[m] + gyu[m + 1], uz, medge[m] + medge[m + 1])
    got = exact_dot(jnp.concatenate([p[rows] for p in parts], axis=0), to_cell[...])
    ux, uy, uz, ue = (got[p * ny:(p + 1) * ny] for p in range(4))
    own_cc[0] = cells(ux)
    own_cc[1] = jnp.concatenate([uy[2:3], uy[6:7]], axis=0)
    own_cc[2] = cells(uz)
    own_cc[3] = cells(ue)

    spot_cc = CC.at[:, i, pl.ds(2 * j, 2), :]
    spot_cb = CB.at[i, pl.ds(2 * j, 2), :]

    def spread(src, dst, which):
        for_others(lambda dev: pltpu.make_async_remote_copy(
            src_ref=src, dst_ref=dst, send_sem=g_send.at[which], recv_sem=g_recv.at[which],
            device_id=dev, device_id_type=MESH,
        ).start())
        pltpu.make_async_copy(src, dst, g_recv.at[which]).start()

    spread(own_cc, spot_cc, 0)

    each(2, "wait_recv")
    v1 = [V1[m] for m in range(nm)]
    v2 = [None] * nm
    for m in range(1, nm - 1):
        around = flow(gxu[m - 1], gxu[m], gyu[m], gzu[m], v1[m - 1], v1[m], v1[m + 1], 2)
        v2[m] = (1.0 + KEEP) * v1[m] + minv[m] * around
    for m in range(2, nm - 2):
        V2[m, rows, :] = v2[m][rows]
    total = None
    for m in range(2, nm - 2):
        around = flow(gxu[m - 1], gxu[m], gyu[m], gzu[m], v2[m - 1], v2[m], v2[m + 1], 2)
        r = mdiag[m] * (v1[m] * (1.0 / OMEGA) - v2[m]) + around
        total = r if total is None else total + r
    own_cb[...] = cells(exact_dot(total[rows], to_cell[...]))
    spread(own_cb, spot_cb, 1)
    each(3, "start")

    pltpu.make_async_copy(CC, CC, g_recv.at[0]).wait()
    cx, cy, cz, ce = CC[0], CC[1], CC[2], CC[3]

    def before(v):
        return jnp.concatenate([v[-1:], v[:-1]], axis=0)

    def after(v):
        return jnp.concatenate([v[1:], v[:1]], axis=0)

    cxl = before(cx)
    cdiag = (cx + cxl) + (cy + shift(cy, 1, 1)) + (cz + shift(cz, 1, 2)) + ce
    cinv = OMEGA * inverse(cdiag)
    cyl, czl = shift(cy, 1, 1) * cinv, shift(cz, 1, 2) * cinv
    cx, cxl, cy, cz = cx * cinv, cxl * cinv, cy * cinv, cz * cinv
    pltpu.make_async_copy(CB, CB, g_recv.at[1]).wait()
    b = CB[...] * cinv
    v = b
    for step in range(SWEEPS - 1):
        around = cxl * before(v) + cx * after(v)
        around = around + cyl * shift(v, 1, 1) + cy * shift(v, -1, 1)
        around = around + czl * shift(v, 1, 2) + cz * shift(v, -1, 2)
        v = KEEP * v + b + around
    CR[1:gx + 1, 8:8 + v.shape[1], :] = v

    near = [CR[i + p, pl.ds(7 + 2 * j + c, 1), :] for p in range(3) for c in range(4)]
    near = exact_dot(jnp.concatenate(near + [jnp.zeros((4, nz // 4), jnp.float32)], axis=0), to_lane[...])
    near = [
        jnp.concatenate([jnp.broadcast_to(near[4 * p + c:4 * p + c + 1], (4, nz)) for c in range(4)], axis=0)
        for p in range(3)
    ]
    each(3, "wait_recv")
    w = [V2[m] + near[m // 2] for m in range(nm)]
    v3 = [None] * nm
    for m in range(1, nm - 1):
        around = flow(gxu[m - 1], gxu[m], gyu[m], gzu[m], w[m - 1], w[m], w[m + 1], 2)
        v3[m] = KEEP * w[m] + v1[m] + minv[m] * around
    f = [None] * nk
    for x in range(2, nk - 2):
        f[x] = u2[x] + v3[(x + 1) // 2]
    for x in range(3, nk - 3):
        around = flow(hx[x - 1], hx[x], hy[x], hz[x], f[x - 1], f[x], f[x + 1], 1)
        out_ref[x - 3] = (KEEP * f[x] + u1[x] + inv[x] * around)[rows]

    for which in range(4):
        each(which, "wait_send")
    pltpu.make_async_copy(bytes_cc, bytes_cc, g_send.at[0]).wait()
    pltpu.make_async_copy(bytes_cb, bytes_cb, g_send.at[1]).wait()


def shards(gx, gy, right_side, labels, conduct_table):
    nx, ny, nz = right_side.shape
    n = gx * gy
    deep = 2 * ROW0 + ny
    cy, cz = gy * (ny // 4), nz // 4
    f32 = jnp.float32
    return pl.pallas_call(
        functools.partial(kernel, gx, gy, nx, ny),
        out_shape=jax.ShapeDtypeStruct(right_side.shape, f32),
        in_specs=[
            pl.BlockSpec(memory_space=pltpu.HBM),
            pl.BlockSpec(memory_space=pltpu.HBM),
            pl.BlockSpec(memory_space=pltpu.HBM),
        ],
        out_specs=pl.BlockSpec(memory_space=pltpu.VMEM),
        scratch_shapes=[
            pltpu.VMEM((nx + 6, deep, nz), f32),
            pltpu.VMEM((nx + 4, deep, nz), f32),
            pltpu.VMEM((nx // 2 + 4, deep, nz), f32),
            pltpu.VMEM((nx // 2 + 4, deep, nz), f32),
            pltpu.VMEM((4, gx, cy, cz), f32),
            pltpu.VMEM((gx, cy, cz), f32),
            pltpu.VMEM((gx + 2, cy + 16, cz), f32),
            pltpu.VMEM((4, 2, cz), f32),
            pltpu.VMEM((2, cz), f32),
            pltpu.VMEM((n - 1, 8, cz), f32),
            pltpu.VMEM((n - 1, 2, cz), f32),
            pltpu.VMEM((nx, ny, nz), jnp.int32),
            pltpu.SMEM((3,), f32),
            pltpu.VMEM((nz, cz), jnp.bfloat16),
            pltpu.VMEM((cz, nz), jnp.bfloat16),
            pltpu.SemaphoreType.DMA((4, 8)),
            pltpu.SemaphoreType.DMA((4, 8)),
            pltpu.SemaphoreType.DMA((2,)),
            pltpu.SemaphoreType.DMA((2,)),
            pltpu.SemaphoreType.DMA((3,)),
        ],
        compiler_params=pltpu.CompilerParams(
            collective_id=0, has_side_effects=True, vmem_limit_bytes=64 * 1024 * 1024
        ),
    )(right_side, labels, conduct_table)


def solution(mesh):
    in_specs = (P("gx", "gy", None), P("gx", "gy", None), P())
    return jax.shard_map(
        functools.partial(shards, mesh.shape["gx"], mesh.shape["gy"]),
        mesh=mesh,
        in_specs=in_specs,
        out_specs=P("gx", "gy", None),
        check_vma=False,
    )
```

```python
import functools

import jax
import jax.numpy as jnp
from jax import lax
from jax.experimental import pallas as pl
from jax.experimental.pallas import tpu as pltpu
from jax.sharding import PartitionSpec as P

SWEEPS = 8
OMEGA = 0.8
KEEP = 1.0 - OMEGA
MESH = pl.DeviceIdType.MESH
TINY = 1e-30

DIRECTIONS = ((1, 0), (-1, 0), (0, 1), (0, -1), (1, 1), (1, -1), (-1, 1), (-1, -1))

ROW0 = 4


def span(step, width, count, first):
    if step == 0:
        return first, first, count
    if step > 0:
        return first + count - width, first - width, width
    return first, first + count, width


def shift(v, by, axis):
    return pltpu.roll(v, by % v.shape[axis], axis)


def flow(low, high, hy, hz, v_low, v, v_high, s):
    a, b = v.ndim - 2, v.ndim - 1
    total = low * v_low + high * v_high
    total = total + hy * shift(v, -s, a) + shift(hy * v, s, a)
    return total + hz * shift(v, -s, b) + shift(hz * v, s, b)


def turn(v, by, axis):
    tile = 8 if axis == 0 else 128
    parts = [lax.slice_in_dim(v, p, p + tile, axis=axis) for p in range(0, v.shape[axis], tile)]
    return jnp.concatenate([pltpu.roll(p, by % tile, axis) for p in parts], axis=axis)


def inverse(d):
    r = pl.reciprocal(d, approx=True)
    return r * (2.0 - d * r)


def harmonic(a, b):
    return (2.0 * (a * b)) * inverse(a + b)


def exact_dot(a, ones):
    rounded = lambda x: x.astype(jnp.bfloat16).astype(jnp.float32)
    head = rounded(a)
    rest = a - head
    middle = rounded(rest)
    parts = jnp.concatenate([head, middle, rest - middle], axis=0).astype(jnp.bfloat16)
    out = jnp.dot(parts, ones, preferred_element_type=jnp.float32)
    n = a.shape[0]
    return out[:n] + out[n:2 * n] + out[2 * n:]


def kernel(gx, gy, nx, ny, rhs_hbm, lab_hbm, tab_hbm, out_ref, K, R, V1, V2, CC, CB, CR, own_cc, own_cb,
           bytes_cy, bytes_cx, bytes_cb, lab_ref, tab_ref, to_cell, to_lane, send, recv, g_send, g_recv, fetch):
    i = lax.axis_index("gx")
    j = lax.axis_index("gy")
    n = gx * gy
    me = i * gy + j
    nz = lab_ref.shape[2]
    mx = nx // 2
    tile = (2 * ROW0 + ny, nz)
    rows = slice(ROW0, ROW0 + ny)

    get_lab = pltpu.make_async_copy(lab_hbm, lab_ref, fetch.at[0])
    get_tab = pltpu.make_async_copy(tab_hbm, tab_ref, fetch.at[1])
    get_rhs = pltpu.make_async_copy(rhs_hbm, R.at[2:2 + nx, rows, :], fetch.at[2])
    get_lab.start()
    get_tab.start()

    K[...] = jnp.full(K.shape, TINY, jnp.float32)
    for buf in (R, V1, V2):
        buf[...] = jnp.zeros(buf.shape, jnp.float32)

    def for_others(what):
        if n <= 64:
            ti = [i] + [lax.rem(i + a, gx) for a in range(1, gx)]
            tj = [j] + [lax.rem(j + b, gy) for b in range(1, gy)]
            for b in reversed(range(gy)):
                for a in range(gx):
                    if a or b:
                        what((ti[a], tj[b]))
        else:
            def one(k, c):
                t = lax.rem(me + k, n)
                what((lax.div(t, gy), lax.rem(t, gy)))
                return c

            lax.fori_loop(1, n, one, 0)

    barrier = pltpu.get_barrier_semaphore()
    for_others(lambda dev: pl.semaphore_signal(barrier, inc=1, device_id=dev, device_id_type=MESH))
    get_rhs.start()

    z = lax.broadcasted_iota(jnp.int32, (nz, nz // 4), 0)
    q = lax.broadcasted_iota(jnp.int32, (nz, nz // 4), 1)
    to_cell[...] = jnp.where(((z >> 2) == q) & ((z & 1) == 0), 1.0, 0.0).astype(jnp.bfloat16)
    q = lax.broadcasted_iota(jnp.int32, (nz // 4, nz), 0)
    z = lax.broadcasted_iota(jnp.int32, (nz // 4, nz), 1)
    to_lane[...] = jnp.where((z >> 2) == q, 1.0, 0.0).astype(jnp.bfloat16)
    CR[...] = jnp.zeros(CR.shape, jnp.float32)

    get_lab.wait()
    get_tab.wait()
    t0, t1, t2 = tab_ref[0], tab_ref[1], tab_ref[2]
    labels = lab_ref[...]
    K[3:3 + nx, rows, :] = jnp.where(labels == 0, t0, jnp.where(labels == 1, t1, t2))
    get_rhs.wait()
    pl.semaphore_wait(barrier, n - 1)

    def there(dx, dy):
        ok = None
        for at, d, size in ((i, dx, gx), (j, dy, gy)):
            if d:
                c = (at < size - 1) if d > 0 else (at > 0)
                ok = c if ok is None else jnp.logical_and(ok, c)
        return ok

    def halo_copy(buf, which, d, x0, cx, y0, cy, wx, wy, corner_x, corner_y):
        dx, dy = DIRECTIONS[d]
        both = dx != 0 and dy != 0
        sx, tx, lx = span(dx, corner_x if both else wx, cx, x0)
        sy, ty, ly = span(dy, corner_y if both else wy, cy, y0)
        return pltpu.make_async_remote_copy(
            src_ref=buf.at[sx:sx + lx, sy:sy + ly, :],
            dst_ref=buf.at[tx:tx + lx, ty:ty + ly, :],
            send_sem=send.at[which, d],
            recv_sem=recv.at[which, d],
            device_id=(i + dx, j + dy),
            device_id_type=MESH,
        )

    halos = {
        0: (K, 3, nx, ROW0, ny, 3, 3, 2, 2),
        1: (R, 2, nx, ROW0, ny, 2, 2, 1, 1),
        2: (V1, 2, mx, ROW0, ny, 2, 4, 1, 2),
        3: (V2, 2, mx, ROW0, ny, 2, 4, 1, 2),
    }

    def each(which, what):
        for d, (dx, dy) in enumerate(DIRECTIONS):
            sign = -1 if what == "wait_recv" else 1

            @pl.when(there(sign * dx, sign * dy))
            def _():
                buf, *sizes = halos[which]
                getattr(halo_copy(buf, which, d, *sizes), what)()

    each(0, "start")
    each(1, "start")

    row = lax.broadcasted_iota(jnp.int32, tile, 0)
    lane = lax.broadcasted_iota(jnp.int32, tile, 1)
    odd_row = (row & 1) == 1
    odd_lane = (lane & 1) == 1
    last_lane = lane == nz - 1
    first_lane = lane == 0

    def pair(v, axis):
        odd = odd_row if axis == 0 else odd_lane
        return v + jnp.where(odd, turn(v, 1, axis), turn(v, -1, axis))

    def upper(v, axis):
        odd = odd_row if axis == 0 else odd_lane
        return jnp.where(odd, v, turn(v, -1, axis))

    one = lambda c: jnp.where(c, 1.0, 0.0)
    faces = one(first_lane) + one(last_lane)
    faces = faces + one((row == ROW0) & (j == 0)) + one((row == ROW0 + ny - 1) & (j == gy - 1))
    x_faces = {3: one(i == 0), 2 + nx: one(i == gx - 1)}

    each(0, "wait_recv")
    nk = nx + 6
    k = [K[x] for x in range(nk)]

    hx = [harmonic(k[x], k[x + 1]) for x in range(nk - 1)]
    hy, hz, edge, diag, inv = ([None] * nk for _ in range(5))
    for x in range(1, nk - 1):
        a = k[x]
        hy[x] = harmonic(a, shift(a, -1, 0))
        hz[x] = harmonic(a, jnp.where(last_lane, 0.0, shift(a, -1, 1)))
        edge[x] = a * ((faces + x_faces[x]) if x in x_faces else faces)
        diag[x] = (hx[x - 1] + hx[x]) + (hy[x] + shift(hy[x], 1, 0)) + (hz[x] + shift(hz[x], 1, 1)) + edge[x]
        inv[x] = OMEGA * inverse(jnp.maximum(diag[x], TINY))

    nm = mx + 4
    gxu = [None] * nm
    gyu, gzu, medge, mdiag, minv = ([None] * nm for _ in range(5))
    for m in range(nm - 1):
        gxu[m] = pair(pair(hx[2 * m], 0), 1)
    for m in range(1, nm - 1):
        x = 2 * m - 1
        gyu[m] = upper(pair(hy[x] + hy[x + 1], 1), 0)
        gzu[m] = upper(pair(hz[x] + hz[x + 1], 0), 1)
        medge[m] = pair(pair(edge[x] + edge[x + 1], 0), 1)
        mdiag[m] = (gxu[m - 1] + gxu[m]) + (gyu[m] + shift(gyu[m], 2, 0))
        mdiag[m] = mdiag[m] + (gzu[m] + shift(gzu[m], 2, 1)) + medge[m]
        minv[m] = OMEGA * inverse(jnp.maximum(mdiag[m], TINY))

    def cells(v):
        return jnp.concatenate([v[0:1] + v[2:3], v[4:5] + v[6:7]], axis=0)

    m = 2
    uz = jnp.where((lane & 2) == 2, gzu[m] + gzu[m + 1], 0.0)
    parts = (gxu[m + 1], gyu[m] + gyu[m + 1], uz, medge[m] + medge[m + 1])
    got = exact_dot(jnp.concatenate([p[rows] for p in parts], axis=0), to_cell[...])
    ux, uy, uz, ue = (got[p * ny:(p + 1) * ny] for p in range(4))
    own_cc[0] = cells(ux)
    own_cc[1] = jnp.concatenate([uy[2:3], uy[6:7]], axis=0)
    own_cc[2] = cells(uz)
    own_cc[3] = cells(ue)

    along_gy = [(i, lax.rem(j + b, gy)) for b in range(1, gy)]
    along_gx = [(lax.rem(i + a, gx), j) for a in range(1, gx)]
    spot_cc = CC.at[:, i, pl.ds(2 * j, 2), :]
    line_cc = CC.at[:, i]

    def to_each(devices, src, dst, which):
        for dev in devices:
            pltpu.make_async_remote_copy(
                src_ref=src, dst_ref=dst, send_sem=g_send.at[which], recv_sem=g_recv.at[which],
                device_id=dev, device_id_type=MESH,
            ).start()

    to_each(along_gy, own_cc, spot_cc, 0)
    pltpu.make_async_copy(own_cc, spot_cc, g_recv.at[0]).start()

    each(1, "wait_recv")
    u1, u2 = [None] * nk, [None] * nk
    for x in range(1, nk - 1):
        u1[x] = R[x - 1] * inv[x]
    for x in range(2, nk - 2):
        around = flow(hx[x - 1], hx[x], hy[x], hz[x], u1[x - 1], u1[x], u1[x + 1], 1)
        u2[x] = (1.0 + KEEP) * u1[x] + inv[x] * around
    res = [None] * nk
    for x in range(3, nk - 3):
        around = flow(hx[x - 1], hx[x], hy[x], hz[x], u2[x - 1], u2[x], u2[x + 1], 1)
        res[x] = diag[x] * (u1[x] * (1.0 / OMEGA) - u2[x]) + around

    for m in range(2, nm - 2):
        x = 2 * m - 1
        source = pair(pair(res[x] + res[x + 1], 0), 1)
        V1[m, rows, :] = (source * minv[m])[rows]
    each(2, "start")

    spot_cb = CB.at[i, pl.ds(2 * j, 2), :]

    pltpu.make_async_copy(line_cc, line_cc, g_recv.at[0]).wait()
    to_each(along_gx, line_cc, line_cc, 1)

    each(2, "wait_recv")
    v1 = [V1[m] for m in range(nm)]
    v2 = [None] * nm
    for m in range(1, nm - 1):
        around = flow(gxu[m - 1], gxu[m], gyu[m], gzu[m], v1[m - 1], v1[m], v1[m + 1], 2)
        v2[m] = (1.0 + KEEP) * v1[m] + minv[m] * around
    for m in range(2, nm - 2):
        V2[m, rows, :] = v2[m][rows]
    total = None
    for m in range(2, nm - 2):
        around = flow(gxu[m - 1], gxu[m], gyu[m], gzu[m], v2[m - 1], v2[m], v2[m + 1], 2)
        r = mdiag[m] * (v1[m] * (1.0 / OMEGA) - v2[m]) + around
        total = r if total is None else total + r
    own_cb[...] = cells(exact_dot(total[rows], to_cell[...]))
    for_others(lambda dev: pltpu.make_async_remote_copy(
        src_ref=own_cb, dst_ref=spot_cb, send_sem=g_send.at[2], recv_sem=g_recv.at[2],
        device_id=dev, device_id_type=MESH,
    ).start())
    pltpu.make_async_copy(own_cb, spot_cb, g_recv.at[2]).start()
    each(3, "start")

    pltpu.make_async_copy(bytes_cx, bytes_cx, g_recv.at[1]).wait()
    cx, cy, cz, ce = CC[0], CC[1], CC[2], CC[3]

    def before(v):
        return jnp.concatenate([v[-1:], v[:-1]], axis=0)

    def after(v):
        return jnp.concatenate([v[1:], v[:1]], axis=0)

    cxl = before(cx)
    cdiag = (cx + cxl) + (cy + shift(cy, 1, 1)) + (cz + shift(cz, 1, 2)) + ce
    cinv = OMEGA * inverse(cdiag)
    cyl, czl = shift(cy, 1, 1) * cinv, shift(cz, 1, 2) * cinv
    cx, cxl, cy, cz = cx * cinv, cxl * cinv, cy * cinv, cz * cinv
    pltpu.make_async_copy(CB, CB, g_recv.at[2]).wait()
    b = CB[...] * cinv
    v = b
    for step in range(SWEEPS - 1):
        around = cxl * before(v) + cx * after(v)
        around = around + cyl * shift(v, 1, 1) + cy * shift(v, -1, 1)
        around = around + czl * shift(v, 1, 2) + cz * shift(v, -1, 2)
        v = KEEP * v + b + around
    CR[1:gx + 1, 8:8 + v.shape[1], :] = v

    near = [CR[i + p, pl.ds(7 + 2 * j + c, 1), :] for p in range(3) for c in range(4)]
    near = exact_dot(jnp.concatenate(near + [jnp.zeros((4, nz // 4), jnp.float32)], axis=0), to_lane[...])
    near = [
        jnp.concatenate([jnp.broadcast_to(near[4 * p + c:4 * p + c + 1], (4, nz)) for c in range(4)], axis=0)
        for p in range(3)
    ]
    each(3, "wait_recv")
    w = [V2[m] + near[m // 2] for m in range(nm)]
    v3 = [None] * nm
    for m in range(1, nm - 1):
        around = flow(gxu[m - 1], gxu[m], gyu[m], gzu[m], w[m - 1], w[m], w[m + 1], 2)
        v3[m] = KEEP * w[m] + v1[m] + minv[m] * around
    f = [None] * nk
    for x in range(2, nk - 2):
        f[x] = u2[x] + v3[(x + 1) // 2]
    for x in range(3, nk - 3):
        around = flow(hx[x - 1], hx[x], hy[x], hz[x], f[x - 1], f[x], f[x + 1], 1)
        out_ref[x - 3] = (KEEP * f[x] + u1[x] + inv[x] * around)[rows]

    for which in range(4):
        each(which, "wait_send")
    for which, amount in enumerate((bytes_cy, bytes_cx, bytes_cb)):
        pltpu.make_async_copy(amount, amount, g_send.at[which]).wait()


def shards(gx, gy, right_side, labels, conduct_table):
    nx, ny, nz = right_side.shape
    n = gx * gy
    deep = 2 * ROW0 + ny
    cy, cz = gy * (ny // 4), nz // 4
    f32 = jnp.float32
    return pl.pallas_call(
        functools.partial(kernel, gx, gy, nx, ny),
        out_shape=jax.ShapeDtypeStruct(right_side.shape, f32),
        in_specs=[
            pl.BlockSpec(memory_space=pltpu.HBM),
            pl.BlockSpec(memory_space=pltpu.HBM),
            pl.BlockSpec(memory_space=pltpu.HBM),
        ],
        out_specs=pl.BlockSpec(memory_space=pltpu.VMEM),
        scratch_shapes=[
            pltpu.VMEM((nx + 6, deep, nz), f32),
            pltpu.VMEM((nx + 4, deep, nz), f32),
            pltpu.VMEM((nx // 2 + 4, deep, nz), f32),
            pltpu.VMEM((nx // 2 + 4, deep, nz), f32),
            pltpu.VMEM((4, gx, cy, cz), f32),
            pltpu.VMEM((gx, cy, cz), f32),
            pltpu.VMEM((gx + 2, cy + 16, cz), f32),
            pltpu.VMEM((4, 2, cz), f32),
            pltpu.VMEM((2, cz), f32),
            pltpu.VMEM((gy - 1, 4, 2, cz), f32),
            pltpu.VMEM((gx - 1, 4, cy, cz), f32),
            pltpu.VMEM((n - 1, 2, cz), f32),
            pltpu.VMEM((nx, ny, nz), jnp.int32),
            pltpu.SMEM((3,), f32),
            pltpu.VMEM((nz, cz), jnp.bfloat16),
            pltpu.VMEM((cz, nz), jnp.bfloat16),
            pltpu.SemaphoreType.DMA((4, 8)),
            pltpu.SemaphoreType.DMA((4, 8)),
            pltpu.SemaphoreType.DMA((3,)),
            pltpu.SemaphoreType.DMA((3,)),
            pltpu.SemaphoreType.DMA((3,)),
        ],
        compiler_params=pltpu.CompilerParams(
            collective_id=0, has_side_effects=True, vmem_limit_bytes=48 * 1024 * 1024
        ),
    )(*(pltpu.with_memory_space_constraint(x, pltpu.HBM) for x in (right_side, labels, conduct_table)))


def solution(mesh):
    in_specs = (P("gx", "gy", None), P("gx", "gy", None), P())
    return jax.shard_map(
        functools.partial(shards, mesh.shape["gx"], mesh.shape["gy"]),
        mesh=mesh,
        in_specs=in_specs,
        out_specs=P("gx", "gy", None),
        check_vma=False,
    )
```

```python
import functools

import jax
import jax.numpy as jnp
from jax import lax
from jax.experimental import pallas as pl
from jax.experimental.pallas import tpu as pltpu
from jax.sharding import PartitionSpec as P

SWEEPS = 8
OMEGA = 0.8
KEEP = 1.0 - OMEGA
MESH = pl.DeviceIdType.MESH
TINY = 1e-30

DIRECTIONS = ((1, 0), (-1, 0), (0, 1), (0, -1), (1, 1), (1, -1), (-1, 1), (-1, -1))

ROW0 = 4


def span(step, width, count, first):
    if step == 0:
        return first, first, count
    if step > 0:
        return first + count - width, first - width, width
    return first, first + count, width


def shift(v, by, axis):
    return pltpu.roll(v, by % v.shape[axis], axis)


def flow(low, high, hy, hz, v_low, v, v_high, s):
    a, b = v.ndim - 2, v.ndim - 1
    total = low * v_low + high * v_high
    total = total + hy * shift(v, -s, a) + shift(hy * v, s, a)
    return total + hz * shift(v, -s, b) + shift(hz * v, s, b)


def turn(v, by, axis):
    tile = 8 if axis == 0 else 128
    parts = [lax.slice_in_dim(v, p, p + tile, axis=axis) for p in range(0, v.shape[axis], tile)]
    return jnp.concatenate([pltpu.roll(p, by % tile, axis) for p in parts], axis=axis)


def inverse(d):
    r = pl.reciprocal(d, approx=True)
    return r * (2.0 - d * r)


def harmonic(a, b):
    return (2.0 * (a * b)) * inverse(a + b)


def exact_dot(a, ones):
    rounded = lambda x: x.astype(jnp.bfloat16).astype(jnp.float32)
    head = rounded(a)
    rest = a - head
    middle = rounded(rest)
    parts = jnp.concatenate([head, middle, rest - middle], axis=0).astype(jnp.bfloat16)
    out = jnp.dot(parts, ones, preferred_element_type=jnp.float32)
    n = a.shape[0]
    return out[:n] + out[n:2 * n] + out[2 * n:]


def kernel(gx, gy, nx, ny, rhs_hbm, lab_hbm, tab_hbm, out_ref, K, R, V1, V2, CC, CB, CR, own_cc, own_cb,
           bytes_cy, bytes_cx, bytes_cb, lab_ref, tab_ref, to_cell, to_lane, send, recv, g_send, g_recv, fetch):
    i = lax.axis_index("gx")
    j = lax.axis_index("gy")
    n = gx * gy
    me = i * gy + j
    nz = lab_ref.shape[2]
    mx = nx // 2
    tile = (2 * ROW0 + ny, nz)
    rows = slice(ROW0, ROW0 + ny)

    get_lab = pltpu.make_async_copy(lab_hbm, lab_ref, fetch.at[0])
    get_tab = pltpu.make_async_copy(tab_hbm, tab_ref, fetch.at[1])
    get_rhs = pltpu.make_async_copy(rhs_hbm, R.at[2:2 + nx, rows, :], fetch.at[2])
    get_lab.start()
    get_tab.start()

    K[...] = jnp.full(K.shape, TINY, jnp.float32)
    for buf in (R, V1, V2):
        buf[...] = jnp.zeros(buf.shape, jnp.float32)

    def for_others(what):
        if n <= 64:
            ti = [i] + [lax.rem(i + a, gx) for a in range(1, gx)]
            tj = [j] + [lax.rem(j + b, gy) for b in range(1, gy)]
            for b in reversed(range(gy)):
                for a in range(gx):
                    if a or b:
                        what((ti[a], tj[b]))
        else:
            def one(k, c):
                t = lax.rem(me + k, n)
                what((lax.div(t, gy), lax.rem(t, gy)))
                return c

            lax.fori_loop(1, n, one, 0)

    barrier = pltpu.get_barrier_semaphore()
    for_others(lambda dev: pl.semaphore_signal(barrier, inc=1, device_id=dev, device_id_type=MESH))
    get_rhs.start()

    z = lax.broadcasted_iota(jnp.int32, (nz, nz // 4), 0)
    q = lax.broadcasted_iota(jnp.int32, (nz, nz // 4), 1)
    to_cell[...] = jnp.where(((z >> 2) == q) & ((z & 1) == 0), 1.0, 0.0).astype(jnp.bfloat16)
    q = lax.broadcasted_iota(jnp.int32, (nz // 4, nz), 0)
    z = lax.broadcasted_iota(jnp.int32, (nz // 4, nz), 1)
    to_lane[...] = jnp.where((z >> 2) == q, 1.0, 0.0).astype(jnp.bfloat16)
    CR[...] = jnp.zeros(CR.shape, jnp.float32)

    get_lab.wait()
    get_tab.wait()
    t0, t1, t2 = tab_ref[0], tab_ref[1], tab_ref[2]
    labels = lab_ref[...]
    K[3:3 + nx, rows, :] = jnp.where(labels == 0, t0, jnp.where(labels == 1, t1, t2))
    get_rhs.wait()
    pl.semaphore_wait(barrier, n - 1)

    def there(dx, dy):
        ok = None
        for at, d, size in ((i, dx, gx), (j, dy, gy)):
            if d:
                c = (at < size - 1) if d > 0 else (at > 0)
                ok = c if ok is None else jnp.logical_and(ok, c)
        return ok

    def halo_copy(buf, which, d, x0, cx, y0, cy, wx, wy, corner_x, corner_y):
        dx, dy = DIRECTIONS[d]
        both = dx != 0 and dy != 0
        sx, tx, lx = span(dx, corner_x if both else wx, cx, x0)
        sy, ty, ly = span(dy, corner_y if both else wy, cy, y0)
        return pltpu.make_async_remote_copy(
            src_ref=buf.at[sx:sx + lx, sy:sy + ly, :],
            dst_ref=buf.at[tx:tx + lx, ty:ty + ly, :],
            send_sem=send.at[which, d],
            recv_sem=recv.at[which, d],
            device_id=(i + dx, j + dy),
            device_id_type=MESH,
        )

    halos = {
        0: (K, 3, nx, ROW0, ny, 3, 3, 2, 2),
        1: (R, 2, nx, ROW0, ny, 2, 2, 1, 1),
        2: (V1, 2, mx, ROW0, ny, 2, 4, 1, 2),
        3: (V2, 2, mx, ROW0, ny, 2, 4, 1, 2),
    }

    def each(which, what):
        for d, (dx, dy) in enumerate(DIRECTIONS):
            sign = -1 if what == "wait_recv" else 1

            @pl.when(there(sign * dx, sign * dy))
            def _():
                buf, *sizes = halos[which]
                getattr(halo_copy(buf, which, d, *sizes), what)()

    each(0, "start")
    each(1, "start")

    row = lax.broadcasted_iota(jnp.int32, tile, 0)
    lane = lax.broadcasted_iota(jnp.int32, tile, 1)
    odd_row = (row & 1) == 1
    odd_lane = (lane & 1) == 1
    last_lane = lane == nz - 1
    first_lane = lane == 0

    def pair(v, axis):
        odd = odd_row if axis == 0 else odd_lane
        return v + jnp.where(odd, turn(v, 1, axis), turn(v, -1, axis))

    def upper(v, axis):
        odd = odd_row if axis == 0 else odd_lane
        return jnp.where(odd, v, turn(v, -1, axis))

    one = lambda c: jnp.where(c, 1.0, 0.0)
    faces = one(first_lane) + one(last_lane)
    faces = faces + one((row == ROW0) & (j == 0)) + one((row == ROW0 + ny - 1) & (j == gy - 1))
    x_faces = {3: one(i == 0), 2 + nx: one(i == gx - 1)}

    each(0, "wait_recv")
    nk = nx + 6
    k = [K[x] for x in range(nk)]

    hx = [harmonic(k[x], k[x + 1]) for x in range(nk - 1)]
    hy, hz, edge, diag, inv = ([None] * nk for _ in range(5))
    for x in range(1, nk - 1):
        a = k[x]
        hy[x] = harmonic(a, shift(a, -1, 0))
        hz[x] = harmonic(a, jnp.where(last_lane, 0.0, shift(a, -1, 1)))
        edge[x] = a * ((faces + x_faces[x]) if x in x_faces else faces)
        diag[x] = (hx[x - 1] + hx[x]) + (hy[x] + shift(hy[x], 1, 0)) + (hz[x] + shift(hz[x], 1, 1)) + edge[x]
        inv[x] = OMEGA * inverse(jnp.maximum(diag[x], TINY))

    nm = mx + 4
    gxu = [None] * nm
    gyu, gzu, medge, mdiag, minv = ([None] * nm for _ in range(5))

    def middle(m):
        x = 2 * m - 1
        for t in (m - 1, m):
            if gxu[t] is None:
                gxu[t] = pair(pair(hx[2 * t], 0), 1)
        gyu[m] = upper(pair(hy[x] + hy[x + 1], 1), 0)
        gzu[m] = upper(pair(hz[x] + hz[x + 1], 0), 1)
        medge[m] = pair(pair(edge[x] + edge[x + 1], 0), 1)
        mdiag[m] = (gxu[m - 1] + gxu[m]) + (gyu[m] + shift(gyu[m], 2, 0))
        mdiag[m] = mdiag[m] + (gzu[m] + shift(gzu[m], 2, 1)) + medge[m]
        minv[m] = OMEGA * inverse(jnp.maximum(mdiag[m], TINY))

    for m in range(2, nm - 2):
        middle(m)

    each(1, "wait_recv")
    u1, u2 = [None] * nk, [None] * nk
    for x in range(1, nk - 1):
        u1[x] = R[x - 1] * inv[x]
    for x in range(2, nk - 2):
        around = flow(hx[x - 1], hx[x], hy[x], hz[x], u1[x - 1], u1[x], u1[x + 1], 1)
        u2[x] = (1.0 + KEEP) * u1[x] + inv[x] * around
    res = [None] * nk
    for x in range(3, nk - 3):
        around = flow(hx[x - 1], hx[x], hy[x], hz[x], u2[x - 1], u2[x], u2[x + 1], 1)
        res[x] = diag[x] * (u1[x] * (1.0 / OMEGA) - u2[x]) + around

    for m in range(2, nm - 2):
        x = 2 * m - 1
        source = pair(pair(res[x] + res[x + 1], 0), 1)
        V1[m, rows, :] = (source * minv[m])[rows]
    each(2, "start")
    for m in (1, nm - 2):
        middle(m)

    def cells(v):
        return jnp.concatenate([v[0:1] + v[2:3], v[4:5] + v[6:7]], axis=0)

    m = 2
    uz = jnp.where((lane & 2) == 2, gzu[m] + gzu[m + 1], 0.0)
    parts = (gxu[m + 1], gyu[m] + gyu[m + 1], uz, medge[m] + medge[m + 1])
    got = exact_dot(jnp.concatenate([p[rows] for p in parts], axis=0), to_cell[...])
    ux, uy, uz, ue = (got[p * ny:(p + 1) * ny] for p in range(4))
    own_cc[0] = cells(ux)
    own_cc[1] = jnp.concatenate([uy[2:3], uy[6:7]], axis=0)
    own_cc[2] = cells(uz)
    own_cc[3] = cells(ue)

    along_gy = [(i, lax.rem(j + b, gy)) for b in range(1, gy)]
    along_gx = [(lax.rem(i + a, gx), j) for a in range(1, gx)]
    spot_cc = CC.at[:, i, pl.ds(2 * j, 2), :]
    line_cc = CC.at[:, i]

    def to_each(devices, src, dst, which):
        for dev in devices:
            pltpu.make_async_remote_copy(
                src_ref=src, dst_ref=dst, send_sem=g_send.at[which], recv_sem=g_recv.at[which],
                device_id=dev, device_id_type=MESH,
            ).start()

    to_each(along_gy, own_cc, spot_cc, 0)
    pltpu.make_async_copy(own_cc, spot_cc, g_recv.at[0]).start()

    spot_cb = CB.at[i, pl.ds(2 * j, 2), :]

    each(2, "wait_recv")
    v1 = [V1[m] for m in range(nm)]
    v2 = [None] * nm
    for m in range(1, nm - 1):
        around = flow(gxu[m - 1], gxu[m], gyu[m], gzu[m], v1[m - 1], v1[m], v1[m + 1], 2)
        v2[m] = (1.0 + KEEP) * v1[m] + minv[m] * around
    for m in range(2, nm - 2):
        V2[m, rows, :] = v2[m][rows]
    pltpu.make_async_copy(line_cc, line_cc, g_recv.at[0]).wait()
    to_each(along_gx, line_cc, line_cc, 1)
    total = None
    for m in range(2, nm - 2):
        around = flow(gxu[m - 1], gxu[m], gyu[m], gzu[m], v2[m - 1], v2[m], v2[m + 1], 2)
        r = mdiag[m] * (v1[m] * (1.0 / OMEGA) - v2[m]) + around
        total = r if total is None else total + r
    own_cb[...] = cells(exact_dot(total[rows], to_cell[...]))
    for_others(lambda dev: pltpu.make_async_remote_copy(
        src_ref=own_cb, dst_ref=spot_cb, send_sem=g_send.at[2], recv_sem=g_recv.at[2],
        device_id=dev, device_id_type=MESH,
    ).start())
    pltpu.make_async_copy(own_cb, spot_cb, g_recv.at[2]).start()
    each(3, "start")

    pltpu.make_async_copy(bytes_cx, bytes_cx, g_recv.at[1]).wait()
    cx, cy, cz, ce = CC[0], CC[1], CC[2], CC[3]

    def before(v):
        return jnp.concatenate([v[-1:], v[:-1]], axis=0)

    def after(v):
        return jnp.concatenate([v[1:], v[:1]], axis=0)

    cxl = before(cx)
    cdiag = (cx + cxl) + (cy + shift(cy, 1, 1)) + (cz + shift(cz, 1, 2)) + ce
    cinv = OMEGA * inverse(cdiag)
    cyl, czl = shift(cy, 1, 1) * cinv, shift(cz, 1, 2) * cinv
    cx, cxl, cy, cz = cx * cinv, cxl * cinv, cy * cinv, cz * cinv
    pltpu.make_async_copy(CB, CB, g_recv.at[2]).wait()
    b = CB[...] * cinv
    v = b
    for step in range(SWEEPS - 1):
        around = cxl * before(v) + cx * after(v)
        around = around + cyl * shift(v, 1, 1) + cy * shift(v, -1, 1)
        around = around + czl * shift(v, 1, 2) + cz * shift(v, -1, 2)
        v = KEEP * v + b + around
    CR[1:gx + 1, 8:8 + v.shape[1], :] = v

    near = [CR[i + p, pl.ds(7 + 2 * j + c, 1), :] for p in range(3) for c in range(4)]
    near = exact_dot(jnp.concatenate(near + [jnp.zeros((4, nz // 4), jnp.float32)], axis=0), to_lane[...])
    near = [
        jnp.concatenate([jnp.broadcast_to(near[4 * p + c:4 * p + c + 1], (4, nz)) for c in range(4)], axis=0)
        for p in range(3)
    ]
    each(3, "wait_recv")
    w = [V2[m] + near[m // 2] for m in range(nm)]
    v3 = [None] * nm
    for m in range(1, nm - 1):
        around = flow(gxu[m - 1], gxu[m], gyu[m], gzu[m], w[m - 1], w[m], w[m + 1], 2)
        v3[m] = KEEP * w[m] + v1[m] + minv[m] * around
    f = [None] * nk
    for x in range(2, nk - 2):
        f[x] = u2[x] + v3[(x + 1) // 2]
    for x in range(3, nk - 3):
        around = flow(hx[x - 1], hx[x], hy[x], hz[x], f[x - 1], f[x], f[x + 1], 1)
        out_ref[x - 3] = (KEEP * f[x] + u1[x] + inv[x] * around)[rows]

    for which in range(4):
        each(which, "wait_send")
    for which, amount in enumerate((bytes_cy, bytes_cx, bytes_cb)):
        pltpu.make_async_copy(amount, amount, g_send.at[which]).wait()


def shards(gx, gy, right_side, labels, conduct_table):
    nx, ny, nz = right_side.shape
    n = gx * gy
    deep = 2 * ROW0 + ny
    cy, cz = gy * (ny // 4), nz // 4
    f32 = jnp.float32
    return pl.pallas_call(
        functools.partial(kernel, gx, gy, nx, ny),
        out_shape=jax.ShapeDtypeStruct(right_side.shape, f32),
        in_specs=[
            pl.BlockSpec(memory_space=pltpu.HBM),
            pl.BlockSpec(memory_space=pltpu.HBM),
            pl.BlockSpec(memory_space=pltpu.HBM),
        ],
        out_specs=pl.BlockSpec(memory_space=pltpu.VMEM),
        scratch_shapes=[
            pltpu.VMEM((nx + 6, deep, nz), f32),
            pltpu.VMEM((nx + 4, deep, nz), f32),
            pltpu.VMEM((nx // 2 + 4, deep, nz), f32),
            pltpu.VMEM((nx // 2 + 4, deep, nz), f32),
            pltpu.VMEM((4, gx, cy, cz), f32),
            pltpu.VMEM((gx, cy, cz), f32),
            pltpu.VMEM((gx + 2, cy + 16, cz), f32),
            pltpu.VMEM((4, 2, cz), f32),
            pltpu.VMEM((2, cz), f32),
            pltpu.VMEM((gy - 1, 4, 2, cz), f32),
            pltpu.VMEM((gx - 1, 4, cy, cz), f32),
            pltpu.VMEM((n - 1, 2, cz), f32),
            pltpu.VMEM((nx, ny, nz), jnp.int32),
            pltpu.SMEM((3,), f32),
            pltpu.VMEM((nz, cz), jnp.bfloat16),
            pltpu.VMEM((cz, nz), jnp.bfloat16),
            pltpu.SemaphoreType.DMA((4, 8)),
            pltpu.SemaphoreType.DMA((4, 8)),
            pltpu.SemaphoreType.DMA((3,)),
            pltpu.SemaphoreType.DMA((3,)),
            pltpu.SemaphoreType.DMA((3,)),
        ],
        compiler_params=pltpu.CompilerParams(
            collective_id=0, has_side_effects=True, vmem_limit_bytes=48 * 1024 * 1024
        ),
    )(*(pltpu.with_memory_space_constraint(x, pltpu.HBM) for x in (right_side, labels, conduct_table)))


def solution(mesh):
    in_specs = (P("gx", "gy", None), P("gx", "gy", None), P())
    return jax.shard_map(
        functools.partial(shards, mesh.shape["gx"], mesh.shape["gy"]),
        mesh=mesh,
        in_specs=in_specs,
        out_specs=P("gx", "gy", None),
        check_vma=False,
    )
```

```python
import functools

import jax
import jax.numpy as jnp
from jax import lax
from jax.experimental import pallas as pl
from jax.experimental.pallas import tpu as pltpu
from jax.sharding import PartitionSpec as P

SWEEPS = 8
OMEGA = 0.8
KEEP = 1.0 - OMEGA
MESH = pl.DeviceIdType.MESH
TINY = 1e-30

DIRECTIONS = ((1, 0), (-1, 0), (0, 1), (0, -1), (1, 1), (1, -1), (-1, 1), (-1, -1))

ROW0 = 4


def span(step, width, count, first):
    if step == 0:
        return first, first, count
    if step > 0:
        return first + count - width, first - width, width
    return first, first + count, width


def shift(v, by, axis):
    return pltpu.roll(v, by % v.shape[axis], axis)


def flow(low, high, hy, hz, v_low, v, v_high, s):
    a, b = v.ndim - 2, v.ndim - 1
    total = low * v_low + high * v_high
    total = total + hy * shift(v, -s, a) + shift(hy * v, s, a)
    return total + hz * shift(v, -s, b) + shift(hz * v, s, b)


def turn(v, by, axis):
    tile = 8 if axis == 0 else 128
    parts = [lax.slice_in_dim(v, p, p + tile, axis=axis) for p in range(0, v.shape[axis], tile)]
    return jnp.concatenate([pltpu.roll(p, by % tile, axis) for p in parts], axis=axis)


def inverse(d):
    r = pl.reciprocal(d, approx=True)
    return r * (2.0 - d * r)


def harmonic(a, b):
    return (2.0 * (a * b)) * inverse(a + b)


def exact_dot(a, ones):
    rounded = lambda x: x.astype(jnp.bfloat16).astype(jnp.float32)
    head = rounded(a)
    rest = a - head
    middle = rounded(rest)
    parts = jnp.concatenate([head, middle, rest - middle], axis=0).astype(jnp.bfloat16)
    out = jnp.dot(parts, ones, preferred_element_type=jnp.float32)
    n = a.shape[0]
    return out[:n] + out[n:2 * n] + out[2 * n:]


def kernel(gx, gy, nx, ny, rhs_hbm, lab_hbm, tab_hbm, out_ref, K, R, V1, V2, CC, CB, CR, own_cc, own_cb,
           bytes_cy, bytes_cx, bytes_cb, lab_ref, tab_ref, to_cell, to_lane, send, recv, g_send, g_recv, fetch, known):
    i = lax.axis_index("gx")
    j = lax.axis_index("gy")
    n = gx * gy
    me = i * gy + j
    nz = lab_ref.shape[2]
    mx = nx // 2
    tile = (2 * ROW0 + ny, nz)
    rows = slice(ROW0, ROW0 + ny)

    get_lab = pltpu.make_async_copy(lab_hbm, lab_ref, fetch.at[0])
    get_tab = pltpu.make_async_copy(tab_hbm, tab_ref, fetch.at[1])
    get_rhs = pltpu.make_async_copy(rhs_hbm, R.at[2:2 + nx, rows, :], fetch.at[2])
    get_lab.start()
    get_tab.start()

    K[...] = jnp.full(K.shape, TINY, jnp.float32)
    for buf in (R, V1, V2):
        buf[...] = jnp.zeros(buf.shape, jnp.float32)

    def for_others(what):
        if n <= 64:
            ti = [i] + [lax.rem(i + a, gx) for a in range(1, gx)]
            tj = [j] + [lax.rem(j + b, gy) for b in range(1, gy)]
            for b in reversed(range(gy)):
                for a in range(gx):
                    if a or b:
                        what((ti[a], tj[b]))
        else:
            def one(k, c):
                t = lax.rem(me + k, n)
                what((lax.div(t, gy), lax.rem(t, gy)))
                return c

            lax.fori_loop(1, n, one, 0)

    def there(dx, dy):
        ok = None
        for at, d, size in ((i, dx, gx), (j, dy, gy)):
            if d:
                c = (at < size - d) if d > 0 else (at >= -d)
                ok = c if ok is None else jnp.logical_and(ok, c)
        return ok

    barrier = pltpu.get_barrier_semaphore()
    for dx, dy in DIRECTIONS:
        @pl.when(there(dx, dy))
        def _():
            pl.semaphore_signal(barrier, inc=1, device_id=(i + dx, j + dy), device_id_type=MESH)

    get_rhs.start()

    z = lax.broadcasted_iota(jnp.int32, (nz, nz // 4), 0)
    q = lax.broadcasted_iota(jnp.int32, (nz, nz // 4), 1)
    to_cell[...] = jnp.where(((z >> 2) == q) & ((z & 1) == 0), 1.0, 0.0).astype(jnp.bfloat16)
    q = lax.broadcasted_iota(jnp.int32, (nz // 4, nz), 0)
    z = lax.broadcasted_iota(jnp.int32, (nz // 4, nz), 1)
    to_lane[...] = jnp.where((z >> 2) == q, 1.0, 0.0).astype(jnp.bfloat16)
    CR[...] = jnp.zeros(CR.shape, jnp.float32)

    get_lab.wait()
    get_tab.wait()
    t0, t1, t2 = tab_ref[0], tab_ref[1], tab_ref[2]
    labels = lab_ref[...]
    K[3:3 + nx, rows, :] = jnp.where(labels == 0, t0, jnp.where(labels == 1, t1, t2))
    get_rhs.wait()
    beside_x = 1 + jnp.where(i > 0, 1, 0) + jnp.where(i < gx - 1, 1, 0)
    beside_y = 1 + jnp.where(j > 0, 1, 0) + jnp.where(j < gy - 1, 1, 0)
    pl.semaphore_wait(barrier, beside_x * beside_y - 1)

    def halo_copy(buf, which, d, x0, cx, y0, cy, wx, wy, corner_x, corner_y):
        dx, dy = DIRECTIONS[d]
        both = dx != 0 and dy != 0
        sx, tx, lx = span(dx, corner_x if both else wx, cx, x0)
        sy, ty, ly = span(dy, corner_y if both else wy, cy, y0)
        return pltpu.make_async_remote_copy(
            src_ref=buf.at[sx:sx + lx, sy:sy + ly, :],
            dst_ref=buf.at[tx:tx + lx, ty:ty + ly, :],
            send_sem=send.at[which, d],
            recv_sem=recv.at[which, d],
            device_id=(i + dx, j + dy),
            device_id_type=MESH,
        )

    halos = {
        0: (K, 3, nx, ROW0, ny, 3, 3, 2, 2),
        1: (R, 2, nx, ROW0, ny, 2, 2, 1, 1),
        2: (V1, 2, mx, ROW0, ny, 2, 4, 1, 2),
        3: (V2, 2, mx, ROW0, ny, 2, 4, 1, 2),
    }

    def each(which, what):
        for d, (dx, dy) in enumerate(DIRECTIONS):
            sign = -1 if what == "wait_recv" else 1

            @pl.when(there(sign * dx, sign * dy))
            def _():
                buf, *sizes = halos[which]
                getattr(halo_copy(buf, which, d, *sizes), what)()

    each(0, "start")
    each(1, "start")

    row = lax.broadcasted_iota(jnp.int32, tile, 0)
    lane = lax.broadcasted_iota(jnp.int32, tile, 1)
    odd_row = (row & 1) == 1
    odd_lane = (lane & 1) == 1
    last_lane = lane == nz - 1
    first_lane = lane == 0

    def pair(v, axis):
        odd = odd_row if axis == 0 else odd_lane
        return v + jnp.where(odd, turn(v, 1, axis), turn(v, -1, axis))

    def upper(v, axis):
        odd = odd_row if axis == 0 else odd_lane
        return jnp.where(odd, v, turn(v, -1, axis))

    one = lambda c: jnp.where(c, 1.0, 0.0)
    faces = one(first_lane) + one(last_lane)
    faces = faces + one((row == ROW0) & (j == 0)) + one((row == ROW0 + ny - 1) & (j == gy - 1))
    x_faces = {3: one(i == 0), 2 + nx: one(i == gx - 1)}

    each(0, "wait_recv")

    steps = [2 << t for t in range(max(gx, gy).bit_length()) if (2 << t) < max(gx, gy) - 1]
    first = [t for t in range(len(steps)) if t == 0 or steps[t] < gy - 1]

    def tell(t):
        for d, (dx, dy) in enumerate(DIRECTIONS):
            dx, dy = dx * steps[t], dy * steps[t]

            @pl.when(there(dx, dy))
            def _():
                pl.semaphore_signal(known.at[t, d], inc=1, device_id=(i + dx, j + dy), device_id_type=MESH)

    def hear(t):
        for d, (dx, dy) in enumerate(DIRECTIONS):
            @pl.when(there(-dx * steps[t], -dy * steps[t]))
            def _():
                pl.semaphore_wait(known.at[t, d], 1)

        if t + 1 < len(steps):
            tell(t + 1)

    if steps:
        tell(0)
    nk = nx + 6
    k = [K[x] for x in range(nk)]

    hx = [harmonic(k[x], k[x + 1]) for x in range(nk - 1)]
    hy, hz, edge, diag, inv = ([None] * nk for _ in range(5))
    for x in range(1, nk - 1):
        a = k[x]
        hy[x] = harmonic(a, shift(a, -1, 0))
        hz[x] = harmonic(a, jnp.where(last_lane, 0.0, shift(a, -1, 1)))
        edge[x] = a * ((faces + x_faces[x]) if x in x_faces else faces)
        diag[x] = (hx[x - 1] + hx[x]) + (hy[x] + shift(hy[x], 1, 0)) + (hz[x] + shift(hz[x], 1, 1)) + edge[x]
        inv[x] = OMEGA * inverse(jnp.maximum(diag[x], TINY))

    nm = mx + 4
    gxu = [None] * nm
    gyu, gzu, medge, mdiag, minv = ([None] * nm for _ in range(5))

    def middle(m):
        x = 2 * m - 1
        for t in (m - 1, m):
            if gxu[t] is None:
                gxu[t] = pair(pair(hx[2 * t], 0), 1)
        gyu[m] = upper(pair(hy[x] + hy[x + 1], 1), 0)
        gzu[m] = upper(pair(hz[x] + hz[x + 1], 0), 1)
        medge[m] = pair(pair(edge[x] + edge[x + 1], 0), 1)
        mdiag[m] = (gxu[m - 1] + gxu[m]) + (gyu[m] + shift(gyu[m], 2, 0))
        mdiag[m] = mdiag[m] + (gzu[m] + shift(gzu[m], 2, 1)) + medge[m]
        minv[m] = OMEGA * inverse(jnp.maximum(mdiag[m], TINY))

    for m in range(2, nm - 2):
        middle(m)

    each(1, "wait_recv")
    u1, u2 = [None] * nk, [None] * nk
    for x in range(1, nk - 1):
        u1[x] = R[x - 1] * inv[x]
    for x in range(2, nk - 2):
        around = flow(hx[x - 1], hx[x], hy[x], hz[x], u1[x - 1], u1[x], u1[x + 1], 1)
        u2[x] = (1.0 + KEEP) * u1[x] + inv[x] * around
    res = [None] * nk
    for x in range(3, nk - 3):
        around = flow(hx[x - 1], hx[x], hy[x], hz[x], u2[x - 1], u2[x], u2[x + 1], 1)
        res[x] = diag[x] * (u1[x] * (1.0 / OMEGA) - u2[x]) + around

    for m in range(2, nm - 2):
        x = 2 * m - 1
        source = pair(pair(res[x] + res[x + 1], 0), 1)
        V1[m, rows, :] = (source * minv[m])[rows]
    each(2, "start")
    for t in range(len(steps)):
        if t in first:
            hear(t)
    for m in (1, nm - 2):
        middle(m)

    def cells(v):
        return jnp.concatenate([v[0:1] + v[2:3], v[4:5] + v[6:7]], axis=0)

    m = 2
    uz = jnp.where((lane & 2) == 2, gzu[m] + gzu[m + 1], 0.0)
    parts = (gxu[m + 1], gyu[m] + gyu[m + 1], uz, medge[m] + medge[m + 1])
    got = exact_dot(jnp.concatenate([p[rows] for p in parts], axis=0), to_cell[...])
    ux, uy, uz, ue = (got[p * ny:(p + 1) * ny] for p in range(4))
    own_cc[0] = cells(ux)
    own_cc[1] = jnp.concatenate([uy[2:3], uy[6:7]], axis=0)
    own_cc[2] = cells(uz)
    own_cc[3] = cells(ue)

    along_gy = [(i, lax.rem(j + b, gy)) for b in range(1, gy)]
    along_gx = [(lax.rem(i + a, gx), j) for a in range(1, gx)]
    spot_cc = CC.at[:, i, pl.ds(2 * j, 2), :]
    line_cc = CC.at[:, i]

    def to_each(devices, src, dst, which):
        for dev in devices:
            pltpu.make_async_remote_copy(
                src_ref=src, dst_ref=dst, send_sem=g_send.at[which], recv_sem=g_recv.at[which],
                device_id=dev, device_id_type=MESH,
            ).start()

    to_each(along_gy, own_cc, spot_cc, 0)
    pltpu.make_async_copy(own_cc, spot_cc, g_recv.at[0]).start()

    spot_cb = CB.at[i, pl.ds(2 * j, 2), :]

    each(2, "wait_recv")
    for t in range(len(steps)):
        if t not in first:
            hear(t)
    v1 = [V1[m] for m in range(nm)]
    v2 = [None] * nm
    for m in range(1, nm - 1):
        around = flow(gxu[m - 1], gxu[m], gyu[m], gzu[m], v1[m - 1], v1[m], v1[m + 1], 2)
        v2[m] = (1.0 + KEEP) * v1[m] + minv[m] * around
    for m in range(2, nm - 2):
        V2[m, rows, :] = v2[m][rows]
    pltpu.make_async_copy(line_cc, line_cc, g_recv.at[0]).wait()
    to_each(along_gx, line_cc, line_cc, 1)
    total = None
    for m in range(2, nm - 2):
        around = flow(gxu[m - 1], gxu[m], gyu[m], gzu[m], v2[m - 1], v2[m], v2[m + 1], 2)
        r = mdiag[m] * (v1[m] * (1.0 / OMEGA) - v2[m]) + around
        total = r if total is None else total + r
    own_cb[...] = cells(exact_dot(total[rows], to_cell[...]))
    for_others(lambda dev: pltpu.make_async_remote_copy(
        src_ref=own_cb, dst_ref=spot_cb, send_sem=g_send.at[2], recv_sem=g_recv.at[2],
        device_id=dev, device_id_type=MESH,
    ).start())
    pltpu.make_async_copy(own_cb, spot_cb, g_recv.at[2]).start()
    each(3, "start")

    pltpu.make_async_copy(bytes_cx, bytes_cx, g_recv.at[1]).wait()
    cx, cy, cz, ce = CC[0], CC[1], CC[2], CC[3]

    def before(v):
        return jnp.concatenate([v[-1:], v[:-1]], axis=0)

    def after(v):
        return jnp.concatenate([v[1:], v[:1]], axis=0)

    cxl = before(cx)
    cdiag = (cx + cxl) + (cy + shift(cy, 1, 1)) + (cz + shift(cz, 1, 2)) + ce
    cinv = OMEGA * inverse(cdiag)
    cyl, czl = shift(cy, 1, 1) * cinv, shift(cz, 1, 2) * cinv
    cx, cxl, cy, cz = cx * cinv, cxl * cinv, cy * cinv, cz * cinv
    pltpu.make_async_copy(CB, CB, g_recv.at[2]).wait()
    b = CB[...] * cinv
    v = b
    for step in range(SWEEPS - 1):
        around = cxl * before(v) + cx * after(v)
        around = around + cyl * shift(v, 1, 1) + cy * shift(v, -1, 1)
        around = around + czl * shift(v, 1, 2) + cz * shift(v, -1, 2)
        v = KEEP * v + b + around
    CR[1:gx + 1, 8:8 + v.shape[1], :] = v

    near = [CR[i + p, pl.ds(7 + 2 * j + c, 1), :] for p in range(3) for c in range(4)]
    near = exact_dot(jnp.concatenate(near + [jnp.zeros((4, nz // 4), jnp.float32)], axis=0), to_lane[...])
    near = [
        jnp.concatenate([jnp.broadcast_to(near[4 * p + c:4 * p + c + 1], (4, nz)) for c in range(4)], axis=0)
        for p in range(3)
    ]
    each(3, "wait_recv")
    w = [V2[m] + near[m // 2] for m in range(nm)]
    v3 = [None] * nm
    for m in range(1, nm - 1):
        around = flow(gxu[m - 1], gxu[m], gyu[m], gzu[m], w[m - 1], w[m], w[m + 1], 2)
        v3[m] = KEEP * w[m] + v1[m] + minv[m] * around
    f = [None] * nk
    for x in range(2, nk - 2):
        f[x] = u2[x] + v3[(x + 1) // 2]
    for x in range(3, nk - 3):
        around = flow(hx[x - 1], hx[x], hy[x], hz[x], f[x - 1], f[x], f[x + 1], 1)
        out_ref[x - 3] = (KEEP * f[x] + u1[x] + inv[x] * around)[rows]

    for which in range(4):
        each(which, "wait_send")
    for which, amount in enumerate((bytes_cy, bytes_cx, bytes_cb)):
        pltpu.make_async_copy(amount, amount, g_send.at[which]).wait()


def shards(gx, gy, right_side, labels, conduct_table):
    nx, ny, nz = right_side.shape
    n = gx * gy
    deep = 2 * ROW0 + ny
    cy, cz = gy * (ny // 4), nz // 4
    f32 = jnp.float32
    return pl.pallas_call(
        functools.partial(kernel, gx, gy, nx, ny),
        out_shape=jax.ShapeDtypeStruct(right_side.shape, f32),
        in_specs=[
            pl.BlockSpec(memory_space=pltpu.HBM),
            pl.BlockSpec(memory_space=pltpu.HBM),
            pl.BlockSpec(memory_space=pltpu.HBM),
        ],
        out_specs=pl.BlockSpec(memory_space=pltpu.VMEM),
        scratch_shapes=[
            pltpu.VMEM((nx + 6, deep, nz), f32),
            pltpu.VMEM((nx + 4, deep, nz), f32),
            pltpu.VMEM((nx // 2 + 4, deep, nz), f32),
            pltpu.VMEM((nx // 2 + 4, deep, nz), f32),
            pltpu.VMEM((4, gx, cy, cz), f32),
            pltpu.VMEM((gx, cy, cz), f32),
            pltpu.VMEM((gx + 2, cy + 16, cz), f32),
            pltpu.VMEM((4, 2, cz), f32),
            pltpu.VMEM((2, cz), f32),
            pltpu.VMEM((gy - 1, 4, 2, cz), f32),
            pltpu.VMEM((gx - 1, 4, cy, cz), f32),
            pltpu.VMEM((n - 1, 2, cz), f32),
            pltpu.VMEM((nx, ny, nz), jnp.int32),
            pltpu.SMEM((3,), f32),
            pltpu.VMEM((nz, cz), jnp.bfloat16),
            pltpu.VMEM((cz, nz), jnp.bfloat16),
            pltpu.SemaphoreType.DMA((4, 8)),
            pltpu.SemaphoreType.DMA((4, 8)),
            pltpu.SemaphoreType.DMA((3,)),
            pltpu.SemaphoreType.DMA((3,)),
            pltpu.SemaphoreType.DMA((3,)),
            pltpu.SemaphoreType.REGULAR((max(gx, gy).bit_length(), 8)),
        ],
        compiler_params=pltpu.CompilerParams(
            collective_id=0, has_side_effects=True, vmem_limit_bytes=48 * 1024 * 1024
        ),
    )(*(pltpu.with_memory_space_constraint(x, pltpu.HBM) for x in (right_side, labels, conduct_table)))


def solution(mesh):
    in_specs = (P("gx", "gy", None), P("gx", "gy", None), P())
    return jax.shard_map(
        functools.partial(shards, mesh.shape["gx"], mesh.shape["gy"]),
        mesh=mesh,
        in_specs=in_specs,
        out_specs=P("gx", "gy", None),
        check_vma=False,
    )
```

```python
import functools

import jax
import jax.numpy as jnp
from jax import lax
from jax.experimental import pallas as pl
from jax.experimental.pallas import tpu as pltpu
from jax.sharding import PartitionSpec as P

SWEEPS = 8
OMEGA = 0.8
KEEP = 1.0 - OMEGA
MESH = pl.DeviceIdType.MESH
TINY = 1e-30

DIRECTIONS = ((1, 0), (-1, 0), (0, 1), (0, -1), (1, 1), (1, -1), (-1, 1), (-1, -1))

ROW0 = 4


def span(step, width, count, first):
    if step == 0:
        return first, first, count
    if step > 0:
        return first + count - width, first - width, width
    return first, first + count, width


def shift(v, by, axis):
    return pltpu.roll(v, by % v.shape[axis], axis)


def flow(low, high, hy, hz, v_low, v, v_high, s):
    a, b = v.ndim - 2, v.ndim - 1
    total = low * v_low + high * v_high
    total = total + hy * shift(v, -s, a) + shift(hy * v, s, a)
    return total + hz * shift(v, -s, b) + shift(hz * v, s, b)


def turn(v, by, axis):
    tile = 8 if axis == 0 else 128
    parts = [lax.slice_in_dim(v, p, p + tile, axis=axis) for p in range(0, v.shape[axis], tile)]
    return jnp.concatenate([pltpu.roll(p, by % tile, axis) for p in parts], axis=axis)


def inverse(d):
    r = pl.reciprocal(d, approx=True)
    return r * (2.0 - d * r)


def harmonic(a, b):
    return (2.0 * (a * b)) * inverse(a + b)


def exact_dot(a, ones):
    rounded = lambda x: x.astype(jnp.bfloat16).astype(jnp.float32)
    head = rounded(a)
    rest = a - head
    middle = rounded(rest)
    parts = jnp.concatenate([head, middle, rest - middle], axis=0).astype(jnp.bfloat16)
    out = jnp.dot(parts, ones, preferred_element_type=jnp.float32)
    n = a.shape[0]
    return out[:n] + out[n:2 * n] + out[2 * n:]


def kernel(gx, gy, nx, ny, rhs_hbm, lab_hbm, tab_hbm, out_ref, K, R, V1, V2, CC, CB, CR, own_cc, own_cb,
           bytes_cy, bytes_cx, bytes_cb, lab_ref, tab_ref, to_cell, to_lane, send, recv, g_send, g_recv, fetch):
    i = lax.axis_index("gx")
    j = lax.axis_index("gy")
    n = gx * gy
    me = i * gy + j
    nz = lab_ref.shape[2]
    mx = nx // 2
    tile = (2 * ROW0 + ny, nz)
    rows = slice(ROW0, ROW0 + ny)

    get_lab = pltpu.make_async_copy(lab_hbm, lab_ref, fetch.at[0])
    get_tab = pltpu.make_async_copy(tab_hbm, tab_ref, fetch.at[1])
    get_rhs = pltpu.make_async_copy(rhs_hbm, R.at[2:2 + nx, rows, :], fetch.at[2])
    get_lab.start()
    get_tab.start()

    K[...] = jnp.full(K.shape, TINY, jnp.float32)
    for buf in (R, V1, V2):
        buf[...] = jnp.zeros(buf.shape, jnp.float32)

    def for_others(what):
        if n <= 64:
            ti = [i] + [lax.rem(i + a, gx) for a in range(1, gx)]
            tj = [j] + [lax.rem(j + b, gy) for b in range(1, gy)]
            for b in reversed(range(gy)):
                for a in range(gx):
                    if a or b:
                        what((ti[a], tj[b]))
        else:
            def one(k, c):
                t = lax.rem(me + k, n)
                what((lax.div(t, gy), lax.rem(t, gy)))
                return c

            lax.fori_loop(1, n, one, 0)

    barrier = pltpu.get_barrier_semaphore()
    for_others(lambda dev: pl.semaphore_signal(barrier, inc=1, device_id=dev, device_id_type=MESH))
    get_rhs.start()

    z = lax.broadcasted_iota(jnp.int32, (nz, nz // 4), 0)
    q = lax.broadcasted_iota(jnp.int32, (nz, nz // 4), 1)
    to_cell[...] = jnp.where(((z >> 2) == q) & ((z & 1) == 0), 1.0, 0.0).astype(jnp.bfloat16)
    q = lax.broadcasted_iota(jnp.int32, (nz // 4, nz), 0)
    z = lax.broadcasted_iota(jnp.int32, (nz // 4, nz), 1)
    to_lane[...] = jnp.where((z >> 2) == q, 1.0, 0.0).astype(jnp.bfloat16)
    CR[...] = jnp.zeros(CR.shape, jnp.float32)

    get_lab.wait()
    get_tab.wait()
    t0, t1, t2 = tab_ref[0], tab_ref[1], tab_ref[2]
    labels = lab_ref[...]
    K[3:3 + nx, rows, :] = jnp.where(labels == 0, t0, jnp.where(labels == 1, t1, t2))
    get_rhs.wait()
    pl.semaphore_wait(barrier, n - 1)

    def there(dx, dy):
        ok = None
        for at, d, size in ((i, dx, gx), (j, dy, gy)):
            if d:
                c = (at < size - 1) if d > 0 else (at > 0)
                ok = c if ok is None else jnp.logical_and(ok, c)
        return ok

    def halo_copy(buf, which, d, x0, cx, y0, cy, wx, wy, corner_x, corner_y):
        dx, dy = DIRECTIONS[d]
        both = dx != 0 and dy != 0
        sx, tx, lx = span(dx, corner_x if both else wx, cx, x0)
        sy, ty, ly = span(dy, corner_y if both else wy, cy, y0)
        return pltpu.make_async_remote_copy(
            src_ref=buf.at[sx:sx + lx, sy:sy + ly, :],
            dst_ref=buf.at[tx:tx + lx, ty:ty + ly, :],
            send_sem=send.at[which, d],
            recv_sem=recv.at[which, d],
            device_id=(i + dx, j + dy),
            device_id_type=MESH,
        )

    halos = {
        0: (K, 3, nx, ROW0, ny, 3, 3, 2, 2),
        1: (R, 2, nx, ROW0, ny, 2, 2, 1, 1),
        2: (V1, 2, mx, ROW0, ny, 2, 4, 1, 2),
        3: (V2, 2, mx, ROW0, ny, 2, 4, 1, 2),
    }

    def each(which, what):
        for d, (dx, dy) in enumerate(DIRECTIONS):
            sign = -1 if what == "wait_recv" else 1

            @pl.when(there(sign * dx, sign * dy))
            def _():
                buf, *sizes = halos[which]
                getattr(halo_copy(buf, which, d, *sizes), what)()

    each(0, "start")
    each(1, "start")

    row = lax.broadcasted_iota(jnp.int32, tile, 0)
    lane = lax.broadcasted_iota(jnp.int32, tile, 1)
    odd_row = (row & 1) == 1
    odd_lane = (lane & 1) == 1
    last_lane = lane == nz - 1
    first_lane = lane == 0

    def pair(v, axis):
        odd = odd_row if axis == 0 else odd_lane
        return v + jnp.where(odd, turn(v, 1, axis), turn(v, -1, axis))

    def upper(v, axis):
        odd = odd_row if axis == 0 else odd_lane
        return jnp.where(odd, v, turn(v, -1, axis))

    one = lambda c: jnp.where(c, 1.0, 0.0)
    faces = one(first_lane) + one(last_lane)
    faces = faces + one((row == ROW0) & (j == 0)) + one((row == ROW0 + ny - 1) & (j == gy - 1))
    x_faces = {3: one(i == 0), 2 + nx: one(i == gx - 1)}

    each(0, "wait_recv")
    nk = nx + 6
    k = [K[x] for x in range(nk)]

    hx = [harmonic(k[x], k[x + 1]) for x in range(nk - 1)]
    hy, hz, edge, diag, inv = ([None] * nk for _ in range(5))
    for x in range(1, nk - 1):
        a = k[x]
        hy[x] = harmonic(a, shift(a, -1, 0))
        hz[x] = harmonic(a, jnp.where(last_lane, 0.0, shift(a, -1, 1)))
        edge[x] = a * ((faces + x_faces[x]) if x in x_faces else faces)
        diag[x] = (hx[x - 1] + hx[x]) + (hy[x] + shift(hy[x], 1, 0)) + (hz[x] + shift(hz[x], 1, 1)) + edge[x]
        inv[x] = OMEGA * inverse(jnp.maximum(diag[x], TINY))

    nm = mx + 4
    gxu = [None] * nm
    gyu, gzu, medge, mdiag, minv = ([None] * nm for _ in range(5))

    def middle(m):
        x = 2 * m - 1
        for t in (m - 1, m):
            if gxu[t] is None:
                gxu[t] = pair(pair(hx[2 * t], 0), 1)
        gyu[m] = upper(pair(hy[x] + hy[x + 1], 1), 0)
        gzu[m] = upper(pair(hz[x] + hz[x + 1], 0), 1)
        medge[m] = pair(pair(edge[x] + edge[x + 1], 0), 1)
        mdiag[m] = (gxu[m - 1] + gxu[m]) + (gyu[m] + shift(gyu[m], 2, 0))
        mdiag[m] = mdiag[m] + (gzu[m] + shift(gzu[m], 2, 1)) + medge[m]
        minv[m] = OMEGA * inverse(jnp.maximum(mdiag[m], TINY))

    for m in range(2, nm - 2):
        middle(m)

    each(1, "wait_recv")
    u1, u2 = [None] * nk, [None] * nk
    for x in range(1, nk - 1):
        u1[x] = R[x - 1] * inv[x]
    for x in range(2, nk - 2):
        around = flow(hx[x - 1], hx[x], hy[x], hz[x], u1[x - 1], u1[x], u1[x + 1], 1)
        u2[x] = (1.0 + KEEP) * u1[x] + inv[x] * around
    res = [None] * nk
    for x in range(3, nk - 3):
        around = flow(hx[x - 1], hx[x], hy[x], hz[x], u2[x - 1], u2[x], u2[x + 1], 1)
        res[x] = diag[x] * (u1[x] * (1.0 / OMEGA) - u2[x]) + around

    for m in range(2, nm - 2):
        x = 2 * m - 1
        source = pair(pair(res[x] + res[x + 1], 0), 1)
        V1[m, rows, :] = (source * minv[m])[rows]
    each(2, "start")
    for m in (1, nm - 2):
        middle(m)

    def cells(v):
        return jnp.concatenate([v[0:1] + v[2:3], v[4:5] + v[6:7]], axis=0)

    m = 2
    uz = jnp.where((lane & 2) == 2, gzu[m] + gzu[m + 1], 0.0)
    parts = (gxu[m + 1], gyu[m] + gyu[m + 1], uz, medge[m] + medge[m + 1])
    got = exact_dot(jnp.concatenate([p[rows] for p in parts], axis=0), to_cell[...])
    ux, uy, uz, ue = (got[p * ny:(p + 1) * ny] for p in range(4))
    own_cc[0] = cells(ux)
    own_cc[1] = jnp.concatenate([uy[2:3], uy[6:7]], axis=0)
    own_cc[2] = cells(uz)
    own_cc[3] = cells(ue)

    along_gy = [(i, lax.rem(j + b, gy)) for b in range(1, gy)]
    along_gx = [(lax.rem(i + a, gx), j) for a in range(1, gx)]
    spot_cc = CC.at[:, i, pl.ds(2 * j, 2), :]
    line_cc = CC.at[:, i]

    def to_each(devices, src, dst, which):
        for dev in devices:
            pltpu.make_async_remote_copy(
                src_ref=src, dst_ref=dst, send_sem=g_send.at[which], recv_sem=g_recv.at[which],
                device_id=dev, device_id_type=MESH,
            ).start()

    to_each(along_gy, own_cc, spot_cc, 0)
    pltpu.make_async_copy(own_cc, spot_cc, g_recv.at[0]).start()

    spot_cb = CB.at[i, pl.ds(2 * j, 2), :]

    each(2, "wait_recv")
    v1 = [V1[m] for m in range(nm)]
    v2 = [None] * nm
    for m in range(1, nm - 1):
        around = flow(gxu[m - 1], gxu[m], gyu[m], gzu[m], v1[m - 1], v1[m], v1[m + 1], 2)
        v2[m] = (1.0 + KEEP) * v1[m] + minv[m] * around
    for m in range(2, nm - 2):
        V2[m, rows, :] = v2[m][rows]
    pltpu.make_async_copy(line_cc, line_cc, g_recv.at[0]).wait()
    to_each(along_gx, line_cc, line_cc, 1)
    total = None
    for m in range(2, nm - 2):
        around = flow(gxu[m - 1], gxu[m], gyu[m], gzu[m], v2[m - 1], v2[m], v2[m + 1], 2)
        r = mdiag[m] * (v1[m] * (1.0 / OMEGA) - v2[m]) + around
        total = r if total is None else total + r
    own_cb[...] = cells(exact_dot(total[rows], to_cell[...]))
    for_others(lambda dev: pltpu.make_async_remote_copy(
        src_ref=own_cb, dst_ref=spot_cb, send_sem=g_send.at[2], recv_sem=g_recv.at[2],
        device_id=dev, device_id_type=MESH,
    ).start())
    pltpu.make_async_copy(own_cb, spot_cb, g_recv.at[2]).start()
    each(3, "start")

    pltpu.make_async_copy(bytes_cx, bytes_cx, g_recv.at[1]).wait()
    cx, cy, cz, ce = CC[0], CC[1], CC[2], CC[3]

    def before(v):
        return jnp.concatenate([v[-1:], v[:-1]], axis=0)

    def after(v):
        return jnp.concatenate([v[1:], v[:1]], axis=0)

    cxl = before(cx)
    cdiag = (cx + cxl) + (cy + shift(cy, 1, 1)) + (cz + shift(cz, 1, 2)) + ce
    cinv = OMEGA * inverse(cdiag)
    cyl, czl = shift(cy, 1, 1) * cinv, shift(cz, 1, 2) * cinv
    cx, cxl, cy, cz = cx * cinv, cxl * cinv, cy * cinv, cz * cinv
    for which in range(3):
        each(which, "wait_send")
    each(3, "wait_recv")
    each(3, "wait_send")
    pltpu.make_async_copy(CB, CB, g_recv.at[2]).wait()
    b = CB[...] * cinv
    v = b
    for step in range(SWEEPS - 1):
        around = cxl * before(v) + cx * after(v)
        around = around + cyl * shift(v, 1, 1) + cy * shift(v, -1, 1)
        around = around + czl * shift(v, 1, 2) + cz * shift(v, -1, 2)
        v = KEEP * v + b + around
    CR[1:gx + 1, 8:8 + v.shape[1], :] = v

    near = [CR[i + p, pl.ds(7 + 2 * j + c, 1), :] for p in range(3) for c in range(4)]
    near = exact_dot(jnp.concatenate(near + [jnp.zeros((4, nz // 4), jnp.float32)], axis=0), to_lane[...])
    near = [
        jnp.concatenate([jnp.broadcast_to(near[4 * p + c:4 * p + c + 1], (4, nz)) for c in range(4)], axis=0)
        for p in range(3)
    ]
    w = [V2[m] + near[m // 2] for m in range(nm)]
    v3 = [None] * nm
    for m in range(1, nm - 1):
        around = flow(gxu[m - 1], gxu[m], gyu[m], gzu[m], w[m - 1], w[m], w[m + 1], 2)
        v3[m] = KEEP * w[m] + v1[m] + minv[m] * around
    f = [None] * nk
    for x in range(2, nk - 2):
        f[x] = u2[x] + v3[(x + 1) // 2]
    for x in range(3, nk - 3):
        around = flow(hx[x - 1], hx[x], hy[x], hz[x], f[x - 1], f[x], f[x + 1], 1)
        out_ref[x - 3] = (KEEP * f[x] + u1[x] + inv[x] * around)[rows]

    for which, amount in enumerate((bytes_cy, bytes_cx, bytes_cb)):
        pltpu.make_async_copy(amount, amount, g_send.at[which]).wait()


def shards(gx, gy, right_side, labels, conduct_table):
    nx, ny, nz = right_side.shape
    n = gx * gy
    deep = 2 * ROW0 + ny
    cy, cz = gy * (ny // 4), nz // 4
    f32 = jnp.float32
    return pl.pallas_call(
        functools.partial(kernel, gx, gy, nx, ny),
        out_shape=jax.ShapeDtypeStruct(right_side.shape, f32),
        in_specs=[
            pl.BlockSpec(memory_space=pltpu.HBM),
            pl.BlockSpec(memory_space=pltpu.HBM),
            pl.BlockSpec(memory_space=pltpu.HBM),
        ],
        out_specs=pl.BlockSpec(memory_space=pltpu.VMEM),
        scratch_shapes=[
            pltpu.VMEM((nx + 6, deep, nz), f32),
            pltpu.VMEM((nx + 4, deep, nz), f32),
            pltpu.VMEM((nx // 2 + 4, deep, nz), f32),
            pltpu.VMEM((nx // 2 + 4, deep, nz), f32),
            pltpu.VMEM((4, gx, cy, cz), f32),
            pltpu.VMEM((gx, cy, cz), f32),
            pltpu.VMEM((gx + 2, cy + 16, cz), f32),
            pltpu.VMEM((4, 2, cz), f32),
            pltpu.VMEM((2, cz), f32),
            pltpu.VMEM((gy - 1, 4, 2, cz), f32),
            pltpu.VMEM((gx - 1, 4, cy, cz), f32),
            pltpu.VMEM((n - 1, 2, cz), f32),
            pltpu.VMEM((nx, ny, nz), jnp.int32),
            pltpu.SMEM((3,), f32),
            pltpu.VMEM((nz, cz), jnp.bfloat16),
            pltpu.VMEM((cz, nz), jnp.bfloat16),
            pltpu.SemaphoreType.DMA((4, 8)),
            pltpu.SemaphoreType.DMA((4, 8)),
            pltpu.SemaphoreType.DMA((3,)),
            pltpu.SemaphoreType.DMA((3,)),
            pltpu.SemaphoreType.DMA((3,)),
        ],
        compiler_params=pltpu.CompilerParams(
            collective_id=0, has_side_effects=True, vmem_limit_bytes=48 * 1024 * 1024
        ),
    )(*(pltpu.with_memory_space_constraint(x, pltpu.HBM) for x in (right_side, labels, conduct_table)))


def solution(mesh):
    in_specs = (P("gx", "gy", None), P("gx", "gy", None), P())
    return jax.shard_map(
        functools.partial(shards, mesh.shape["gx"], mesh.shape["gy"]),
        mesh=mesh,
        in_specs=in_specs,
        out_specs=P("gx", "gy", None),
        check_vma=False,
    )
```

```python
import functools

import jax
import jax.numpy as jnp
from jax import lax
from jax.experimental import pallas as pl
from jax.experimental.pallas import tpu as pltpu
from jax.sharding import PartitionSpec as P

SWEEPS = 8
OMEGA = 0.8
KEEP = 1.0 - OMEGA
MESH = pl.DeviceIdType.MESH
TINY = 1e-30

DIRECTIONS = ((1, 0), (-1, 0), (0, 1), (0, -1), (1, 1), (1, -1), (-1, 1), (-1, -1))

ROW0 = 4


def span(step, width, count, first):
    if step == 0:
        return first, first, count
    if step > 0:
        return first + count - width, first - width, width
    return first, first + count, width


def shift(v, by, axis):
    return pltpu.roll(v, by % v.shape[axis], axis)


def flow(low, high, hy, hz, v_low, v, v_high, s):
    a, b = v.ndim - 2, v.ndim - 1
    total = low * v_low + high * v_high
    total = total + hy * shift(v, -s, a) + shift(hy * v, s, a)
    return total + hz * shift(v, -s, b) + shift(hz * v, s, b)


def turn(v, by, axis):
    tile = 8 if axis == 0 else 128
    parts = [lax.slice_in_dim(v, p, p + tile, axis=axis) for p in range(0, v.shape[axis], tile)]
    return jnp.concatenate([pltpu.roll(p, by % tile, axis) for p in parts], axis=axis)


def inverse(d):
    r = pl.reciprocal(d, approx=True)
    return r * (2.0 - d * r)


def harmonic(a, b):
    return (2.0 * (a * b)) * inverse(a + b)


def exact_dot(a, ones):
    rounded = lambda x: x.astype(jnp.bfloat16).astype(jnp.float32)
    head = rounded(a)
    rest = a - head
    middle = rounded(rest)
    parts = jnp.concatenate([head, middle, rest - middle], axis=0).astype(jnp.bfloat16)
    out = jnp.dot(parts, ones, preferred_element_type=jnp.float32)
    n = a.shape[0]
    return out[:n] + out[n:2 * n] + out[2 * n:]


def kernel(gx, gy, nx, ny, rhs_hbm, lab_hbm, tab_hbm, out_ref, K, R, V1, V2, CC, CB, CR, own_cc, own_cb,
           bytes_cy, bytes_cx, bytes_cb, lab_ref, tab_ref, to_cell, to_lane, send, recv, g_send, g_recv, fetch,
           HX, HY, HZ, EDGE, DIAG, INV, U1, U2, U3, GX, GY, GZ, MEDGE, MDIAG, MINV, T):
    i = lax.axis_index("gx")
    j = lax.axis_index("gy")
    n = gx * gy
    me = i * gy + j
    nz = lab_ref.shape[2]
    mx = nx // 2
    tile = (2 * ROW0 + ny, nz)
    rows = slice(ROW0, ROW0 + ny)

    get_lab = pltpu.make_async_copy(lab_hbm, lab_ref, fetch.at[0])
    get_tab = pltpu.make_async_copy(tab_hbm, tab_ref, fetch.at[1])
    get_rhs = pltpu.make_async_copy(rhs_hbm, R.at[2:2 + nx, rows, :], fetch.at[2])
    get_lab.start()
    get_tab.start()

    K[...] = jnp.full(K.shape, TINY, jnp.float32)
    for buf in (R, V1, V2):
        buf[...] = jnp.zeros(buf.shape, jnp.float32)

    def for_others(what):
        if n <= 64:
            ti = [i] + [lax.rem(i + a, gx) for a in range(1, gx)]
            tj = [j] + [lax.rem(j + b, gy) for b in range(1, gy)]
            for b in reversed(range(gy)):
                for a in range(gx):
                    if a or b:
                        what((ti[a], tj[b]))
        else:
            def one(k, c):
                t = lax.rem(me + k, n)
                what((lax.div(t, gy), lax.rem(t, gy)))
                return c

            lax.fori_loop(1, n, one, 0)

    barrier = pltpu.get_barrier_semaphore()
    for_others(lambda dev: pl.semaphore_signal(barrier, inc=1, device_id=dev, device_id_type=MESH))
    get_rhs.start()

    z = lax.broadcasted_iota(jnp.int32, (nz, nz // 4), 0)
    q = lax.broadcasted_iota(jnp.int32, (nz, nz // 4), 1)
    to_cell[...] = jnp.where(((z >> 2) == q) & ((z & 1) == 0), 1.0, 0.0).astype(jnp.bfloat16)
    q = lax.broadcasted_iota(jnp.int32, (nz // 4, nz), 0)
    z = lax.broadcasted_iota(jnp.int32, (nz // 4, nz), 1)
    to_lane[...] = jnp.where((z >> 2) == q, 1.0, 0.0).astype(jnp.bfloat16)
    CR[...] = jnp.zeros(CR.shape, jnp.float32)

    get_lab.wait()
    get_tab.wait()
    t0, t1, t2 = tab_ref[0], tab_ref[1], tab_ref[2]
    labels = lab_ref[...]
    K[3:3 + nx, rows, :] = jnp.where(labels == 0, t0, jnp.where(labels == 1, t1, t2))
    get_rhs.wait()
    pl.semaphore_wait(barrier, n - 1)

    def there(dx, dy):
        ok = None
        for at, d, size in ((i, dx, gx), (j, dy, gy)):
            if d:
                c = (at < size - 1) if d > 0 else (at > 0)
                ok = c if ok is None else jnp.logical_and(ok, c)
        return ok

    def halo_copy(buf, which, d, x0, cx, y0, cy, wx, wy, corner_x, corner_y):
        dx, dy = DIRECTIONS[d]
        both = dx != 0 and dy != 0
        sx, tx, lx = span(dx, corner_x if both else wx, cx, x0)
        sy, ty, ly = span(dy, corner_y if both else wy, cy, y0)
        return pltpu.make_async_remote_copy(
            src_ref=buf.at[sx:sx + lx, sy:sy + ly, :],
            dst_ref=buf.at[tx:tx + lx, ty:ty + ly, :],
            send_sem=send.at[which, d],
            recv_sem=recv.at[which, d],
            device_id=(i + dx, j + dy),
            device_id_type=MESH,
        )

    halos = {
        0: (K, 3, nx, ROW0, ny, 3, 3, 2, 2),
        1: (R, 2, nx, ROW0, ny, 2, 2, 1, 1),
        2: (V1, 2, mx, ROW0, ny, 2, 4, 1, 2),
        3: (V2, 2, mx, ROW0, ny, 2, 4, 1, 2),
    }

    def each(which, what):
        for d, (dx, dy) in enumerate(DIRECTIONS):
            sign = -1 if what == "wait_recv" else 1

            @pl.when(there(sign * dx, sign * dy))
            def _():
                buf, *sizes = halos[which]
                getattr(halo_copy(buf, which, d, *sizes), what)()

    each(0, "start")
    each(1, "start")

    row = lax.broadcasted_iota(jnp.int32, tile, 0)
    lane = lax.broadcasted_iota(jnp.int32, tile, 1)
    odd_row = (row & 1) == 1
    odd_lane = (lane & 1) == 1
    last_lane = lane == nz - 1
    first_lane = lane == 0

    def pair(v, axis):
        odd = odd_row if axis == 0 else odd_lane
        return v + jnp.where(odd, turn(v, 1, axis), turn(v, -1, axis))

    def upper(v, axis):
        odd = odd_row if axis == 0 else odd_lane
        return jnp.where(odd, v, turn(v, -1, axis))

    one = lambda c: jnp.where(c, 1.0, 0.0)
    faces = one(first_lane) + one(last_lane)
    faces = faces + one((row == ROW0) & (j == 0)) + one((row == ROW0 + ny - 1) & (j == gy - 1))
    x_low, x_high = one(i == 0), one(i == gx - 1)

    def over(first, last, body):
        def step(x, c):
            body(x)
            return c

        lax.fori_loop(first, last, step, 0)

    each(0, "wait_recv")
    nk = nx + 6
    HX[0] = harmonic(K[0], K[1])

    def fine(x):
        a = K[x]
        high = harmonic(a, K[x + 1])
        hy = harmonic(a, shift(a, -1, 0))
        hz = harmonic(a, jnp.where(last_lane, 0.0, shift(a, -1, 1)))
        edge = a * (faces + (jnp.where(x == 3, x_low, 0.0) + jnp.where(x == 2 + nx, x_high, 0.0)))
        diag = (HX[x - 1] + high) + (hy + shift(hy, 1, 0)) + (hz + shift(hz, 1, 1)) + edge
        HX[x], HY[x], HZ[x], EDGE[x], DIAG[x] = high, hy, hz, edge, diag
        INV[x] = OMEGA * inverse(jnp.maximum(diag, TINY))

    over(1, nk - 1, fine)

    nm = mx + 4
    GX[0] = pair(pair(HX[0], 0), 1)

    def middle(m):
        x = 2 * m - 1
        gx_high = pair(pair(HX[x + 1], 0), 1)
        gyu = upper(pair(HY[x] + HY[x + 1], 1), 0)
        gzu = upper(pair(HZ[x] + HZ[x + 1], 0), 1)
        edge = pair(pair(EDGE[x] + EDGE[x + 1], 0), 1)
        diag = (GX[m - 1] + gx_high) + (gyu + shift(gyu, 2, 0)) + (gzu + shift(gzu, 2, 1)) + edge
        GX[m], GY[m], GZ[m], MEDGE[m], MDIAG[m] = gx_high, gyu, gzu, edge, diag
        MINV[m] = OMEGA * inverse(jnp.maximum(diag, TINY))

    over(1, nm - 1, middle)

    each(1, "wait_recv")

    def source(x):
        U1[x] = R[x - 1] * INV[x]

    def fine_flow(x, v):
        return flow(HX[x - 1], HX[x], HY[x], HZ[x], v[x - 1], v[x], v[x + 1], 1)

    def middle_flow(m, v):
        return flow(GX[m - 1], GX[m], GY[m], GZ[m], v[m - 1], v[m], v[m + 1], 2)

    def second(x):
        U2[x] = (1.0 + KEEP) * U1[x] + INV[x] * fine_flow(x, U1)

    def residual(x):
        return DIAG[x] * (U1[x] * (1.0 / OMEGA) - U2[x]) + fine_flow(x, U2)

    def restricted(m):
        x = 2 * m - 1
        V1[m, rows, :] = (pair(pair(residual(x) + residual(x + 1), 0), 1) * MINV[m])[rows]

    over(1, nk - 1, source)
    over(2, nk - 2, second)
    over(2, nm - 2, restricted)
    each(2, "start")
    def cells(v):
        return jnp.concatenate([v[0:1] + v[2:3], v[4:5] + v[6:7]], axis=0)

    m = 2
    uz = jnp.where((lane & 2) == 2, GZ[m] + GZ[m + 1], 0.0)
    parts = (GX[m + 1], GY[m] + GY[m + 1], uz, MEDGE[m] + MEDGE[m + 1])
    got = exact_dot(jnp.concatenate([p[rows] for p in parts], axis=0), to_cell[...])
    ux, uy, uz, ue = (got[p * ny:(p + 1) * ny] for p in range(4))
    own_cc[0] = cells(ux)
    own_cc[1] = jnp.concatenate([uy[2:3], uy[6:7]], axis=0)
    own_cc[2] = cells(uz)
    own_cc[3] = cells(ue)

    along_gy = [(i, lax.rem(j + b, gy)) for b in range(1, gy)]
    along_gx = [(lax.rem(i + a, gx), j) for a in range(1, gx)]
    spot_cc = CC.at[:, i, pl.ds(2 * j, 2), :]
    line_cc = CC.at[:, i]

    def to_each(devices, src, dst, which):
        for dev in devices:
            pltpu.make_async_remote_copy(
                src_ref=src, dst_ref=dst, send_sem=g_send.at[which], recv_sem=g_recv.at[which],
                device_id=dev, device_id_type=MESH,
            ).start()

    to_each(along_gy, own_cc, spot_cc, 0)
    pltpu.make_async_copy(own_cc, spot_cc, g_recv.at[0]).start()

    spot_cb = CB.at[i, pl.ds(2 * j, 2), :]

    each(2, "wait_recv")

    def middle_second(m):
        T[m] = (1.0 + KEEP) * V1[m] + MINV[m] * middle_flow(m, V1)

    over(1, nm - 1, middle_second)
    V2[2:nm - 2, rows, :] = T[2:nm - 2, rows, :]
    pltpu.make_async_copy(line_cc, line_cc, g_recv.at[0]).wait()
    to_each(along_gx, line_cc, line_cc, 1)

    def middle_residual(m, total):
        return total + MDIAG[m] * (V1[m] * (1.0 / OMEGA) - T[m]) + middle_flow(m, T)

    total = lax.fori_loop(2, nm - 2, middle_residual, jnp.zeros(tile, jnp.float32))
    own_cb[...] = cells(exact_dot(total[rows], to_cell[...]))
    for_others(lambda dev: pltpu.make_async_remote_copy(
        src_ref=own_cb, dst_ref=spot_cb, send_sem=g_send.at[2], recv_sem=g_recv.at[2],
        device_id=dev, device_id_type=MESH,
    ).start())
    pltpu.make_async_copy(own_cb, spot_cb, g_recv.at[2]).start()
    each(3, "start")

    pltpu.make_async_copy(bytes_cx, bytes_cx, g_recv.at[1]).wait()
    cx, cy, cz, ce = CC[0], CC[1], CC[2], CC[3]

    def before(v):
        return jnp.concatenate([v[-1:], v[:-1]], axis=0)

    def after(v):
        return jnp.concatenate([v[1:], v[:1]], axis=0)

    cxl = before(cx)
    cdiag = (cx + cxl) + (cy + shift(cy, 1, 1)) + (cz + shift(cz, 1, 2)) + ce
    cinv = OMEGA * inverse(cdiag)
    cyl, czl = shift(cy, 1, 1) * cinv, shift(cz, 1, 2) * cinv
    cx, cxl, cy, cz = cx * cinv, cxl * cinv, cy * cinv, cz * cinv
    for which in range(3):
        each(which, "wait_send")
    each(3, "wait_recv")
    each(3, "wait_send")
    pltpu.make_async_copy(CB, CB, g_recv.at[2]).wait()
    b = CB[...] * cinv

    def coarse(step, v):
        around = cxl * before(v) + cx * after(v)
        around = around + cyl * shift(v, 1, 1) + cy * shift(v, -1, 1)
        around = around + czl * shift(v, 1, 2) + cz * shift(v, -1, 2)
        return KEEP * v + b + around

    v = lax.fori_loop(1, SWEEPS, coarse, b)
    CR[1:gx + 1, 8:8 + v.shape[1], :] = v

    near = [CR[i + p, pl.ds(7 + 2 * j + c, 1), :] for p in range(3) for c in range(4)]
    near = exact_dot(jnp.concatenate(near + [jnp.zeros((4, nz // 4), jnp.float32)], axis=0), to_lane[...])
    near = [
        jnp.concatenate([jnp.broadcast_to(near[4 * p + c:4 * p + c + 1], (4, nz)) for c in range(4)], axis=0)
        for p in range(3)
    ]
    for m in range(nm):
        T[m] = V2[m] + near[m // 2]

    def middle_up(m):
        v3 = KEEP * T[m] + V1[m] + MINV[m] * middle_flow(m, T)
        U3[2 * m - 1] = U2[2 * m - 1] + v3
        U3[2 * m] = U2[2 * m] + v3

    def fine_up(x):
        out_ref[x - 3] = (KEEP * U3[x] + U1[x] + INV[x] * fine_flow(x, U3))[rows]

    over(1, nm - 1, middle_up)
    over(3, nk - 3, fine_up)

    for which, amount in enumerate((bytes_cy, bytes_cx, bytes_cb)):
        pltpu.make_async_copy(amount, amount, g_send.at[which]).wait()


def shards(gx, gy, right_side, labels, conduct_table):
    nx, ny, nz = right_side.shape
    n = gx * gy
    deep = 2 * ROW0 + ny
    cy, cz = gy * (ny // 4), nz // 4
    f32 = jnp.float32
    return pl.pallas_call(
        functools.partial(kernel, gx, gy, nx, ny),
        out_shape=jax.ShapeDtypeStruct(right_side.shape, f32),
        in_specs=[
            pl.BlockSpec(memory_space=pltpu.HBM),
            pl.BlockSpec(memory_space=pltpu.HBM),
            pl.BlockSpec(memory_space=pltpu.HBM),
        ],
        out_specs=pl.BlockSpec(memory_space=pltpu.VMEM),
        scratch_shapes=[
            pltpu.VMEM((nx + 6, deep, nz), f32),
            pltpu.VMEM((nx + 4, deep, nz), f32),
            pltpu.VMEM((nx // 2 + 4, deep, nz), f32),
            pltpu.VMEM((nx // 2 + 4, deep, nz), f32),
            pltpu.VMEM((4, gx, cy, cz), f32),
            pltpu.VMEM((gx, cy, cz), f32),
            pltpu.VMEM((gx + 2, cy + 16, cz), f32),
            pltpu.VMEM((4, 2, cz), f32),
            pltpu.VMEM((2, cz), f32),
            pltpu.VMEM((gy - 1, 4, 2, cz), f32),
            pltpu.VMEM((gx - 1, 4, cy, cz), f32),
            pltpu.VMEM((n - 1, 2, cz), f32),
            pltpu.VMEM((nx, ny, nz), jnp.int32),
            pltpu.SMEM((3,), f32),
            pltpu.VMEM((nz, cz), jnp.bfloat16),
            pltpu.VMEM((cz, nz), jnp.bfloat16),
            pltpu.SemaphoreType.DMA((4, 8)),
            pltpu.SemaphoreType.DMA((4, 8)),
            pltpu.SemaphoreType.DMA((3,)),
            pltpu.SemaphoreType.DMA((3,)),
            pltpu.SemaphoreType.DMA((3,)),
        ] + [pltpu.VMEM((nx + 6, deep, nz), f32)] * 9 + [pltpu.VMEM((nx // 2 + 4, deep, nz), f32)] * 7,
        compiler_params=pltpu.CompilerParams(
            collective_id=0, has_side_effects=True, vmem_limit_bytes=48 * 1024 * 1024
        ),
    )(*(pltpu.with_memory_space_constraint(x, pltpu.HBM) for x in (right_side, labels, conduct_table)))


def solution(mesh):
    in_specs = (P("gx", "gy", None), P("gx", "gy", None), P())
    return jax.shard_map(
        functools.partial(shards, mesh.shape["gx"], mesh.shape["gy"]),
        mesh=mesh,
        in_specs=in_specs,
        out_specs=P("gx", "gy", None),
        check_vma=False,
    )
```

```python
import functools

import jax
import jax.numpy as jnp
from jax import lax
from jax.experimental import pallas as pl
from jax.experimental.pallas import tpu as pltpu
from jax.sharding import PartitionSpec as P

SWEEPS = 8
OMEGA = 0.8
KEEP = 1.0 - OMEGA
MESH = pl.DeviceIdType.MESH
TINY = 1e-30

DIRECTIONS = ((1, 0), (-1, 0), (0, 1), (0, -1), (1, 1), (1, -1), (-1, 1), (-1, -1))

ROW0 = 4


def span(step, width, count, first):
    if step == 0:
        return first, first, count
    if step > 0:
        return first + count - width, first - width, width
    return first, first + count, width


def shift(v, by, axis):
    return pltpu.roll(v, by % v.shape[axis], axis)


def flow(low, high, hy, hz, v_low, v, v_high, s):
    a, b = v.ndim - 2, v.ndim - 1
    total = low * v_low + high * v_high
    total = total + hy * shift(v, -s, a) + shift(hy * v, s, a)
    return total + hz * shift(v, -s, b) + shift(hz * v, s, b)


def turn(v, by, axis):
    tile = 8 if axis == 0 else 128
    parts = [lax.slice_in_dim(v, p, p + tile, axis=axis) for p in range(0, v.shape[axis], tile)]
    return jnp.concatenate([pltpu.roll(p, by % tile, axis) for p in parts], axis=axis)


def inverse(d):
    r = pl.reciprocal(d, approx=True)
    return r * (2.0 - d * r)


def harmonic(a, b):
    return (2.0 * (a * b)) * inverse(a + b)


def exact_dot(a, ones):
    rounded = lambda x: x.astype(jnp.bfloat16).astype(jnp.float32)
    head = rounded(a)
    rest = a - head
    middle = rounded(rest)
    parts = jnp.concatenate([head, middle, rest - middle], axis=0).astype(jnp.bfloat16)
    out = jnp.dot(parts, ones, preferred_element_type=jnp.float32)
    n = a.shape[0]
    return out[:n] + out[n:2 * n] + out[2 * n:]


def kernel(gx, gy, nx, ny, rhs_hbm, lab_hbm, tab_hbm, out_ref, L, R, V1, V2, CC, CB, CR, own_cc, own_cb,
           bytes_cy, bytes_cx, bytes_cb, tab_ref, to_cell, to_lane, send, recv, g_send, g_recv, fetch):
    i = lax.axis_index("gx")
    j = lax.axis_index("gy")
    n = gx * gy
    me = i * gy + j
    nz = L.shape[2]
    mx = nx // 2
    tile = (2 * ROW0 + ny, nz)
    rows = slice(ROW0, ROW0 + ny)

    get_lab = pltpu.make_async_copy(lab_hbm, L.at[3:3 + nx, rows, :], fetch.at[0])
    get_tab = pltpu.make_async_copy(tab_hbm, tab_ref, fetch.at[1])
    get_rhs = pltpu.make_async_copy(rhs_hbm, R.at[2:2 + nx, rows, :], fetch.at[2])
    get_tab.start()

    L[...] = jnp.full(L.shape, -1, jnp.int32)
    for buf in (R, V1, V2):
        buf[...] = jnp.zeros(buf.shape, jnp.float32)

    def for_others(what):
        if n <= 64:
            ti = [i] + [lax.rem(i + a, gx) for a in range(1, gx)]
            tj = [j] + [lax.rem(j + b, gy) for b in range(1, gy)]
            for b in reversed(range(gy)):
                for a in range(gx):
                    if a or b:
                        what((ti[a], tj[b]))
        else:
            def one(k, c):
                t = lax.rem(me + k, n)
                what((lax.div(t, gy), lax.rem(t, gy)))
                return c

            lax.fori_loop(1, n, one, 0)

    barrier = pltpu.get_barrier_semaphore()
    for_others(lambda dev: pl.semaphore_signal(barrier, inc=1, device_id=dev, device_id_type=MESH))
    get_lab.start()
    get_rhs.start()

    pl.semaphore_wait(barrier, n - 1)

    def there(dx, dy):
        ok = None
        for at, d, size in ((i, dx, gx), (j, dy, gy)):
            if d:
                c = (at < size - 1) if d > 0 else (at > 0)
                ok = c if ok is None else jnp.logical_and(ok, c)
        return ok

    def halo_copy(buf, whole, which, d, x0, cx, y0, cy, wx, wy, corner_x, corner_y):
        dx, dy = DIRECTIONS[d]
        both = dx != 0 and dy != 0
        sx, tx, lx = span(dx, corner_x if both else wx, cx, x0)
        sy, ty, ly = span(dy, corner_y if both else wy, cy, y0)
        return pltpu.make_async_remote_copy(
            src_ref=(
                buf.at[sx:sx + lx, sy:sy + ly, :] if whole is None
                else whole.at[sx - x0:sx - x0 + lx, sy - y0:sy - y0 + ly, :]
            ),
            dst_ref=buf.at[tx:tx + lx, ty:ty + ly, :],
            send_sem=send.at[which, d],
            recv_sem=recv.at[which, d],
            device_id=(i + dx, j + dy),
            device_id_type=MESH,
        )

    halos = {
        0: (L, lab_hbm, 3, nx, ROW0, ny, 3, 3, 2, 2),
        1: (R, rhs_hbm, 2, nx, ROW0, ny, 2, 2, 1, 1),
        2: (V1, None, 2, mx, ROW0, ny, 2, 4, 1, 2),
        3: (V2, None, 2, mx, ROW0, ny, 2, 4, 1, 2),
    }

    def each(which, what):
        for d, (dx, dy) in enumerate(DIRECTIONS):
            sign = -1 if what == "wait_recv" else 1

            @pl.when(there(sign * dx, sign * dy))
            def _():
                buf, whole, *sizes = halos[which]
                getattr(halo_copy(buf, whole, which, d, *sizes), what)()

    each(0, "start")
    each(1, "start")

    z = lax.broadcasted_iota(jnp.int32, (nz, nz // 4), 0)
    q = lax.broadcasted_iota(jnp.int32, (nz, nz // 4), 1)
    to_cell[...] = jnp.where(((z >> 2) == q) & ((z & 1) == 0), 1.0, 0.0).astype(jnp.bfloat16)
    q = lax.broadcasted_iota(jnp.int32, (nz // 4, nz), 0)
    z = lax.broadcasted_iota(jnp.int32, (nz // 4, nz), 1)
    to_lane[...] = jnp.where((z >> 2) == q, 1.0, 0.0).astype(jnp.bfloat16)
    CR[...] = jnp.zeros(CR.shape, jnp.float32)

    row = lax.broadcasted_iota(jnp.int32, tile, 0)
    lane = lax.broadcasted_iota(jnp.int32, tile, 1)
    odd_row = (row & 1) == 1
    odd_lane = (lane & 1) == 1
    last_lane = lane == nz - 1
    first_lane = lane == 0

    def pair(v, axis):
        odd = odd_row if axis == 0 else odd_lane
        return v + jnp.where(odd, turn(v, 1, axis), turn(v, -1, axis))

    def upper(v, axis):
        odd = odd_row if axis == 0 else odd_lane
        return jnp.where(odd, v, turn(v, -1, axis))

    one = lambda c: jnp.where(c, 1.0, 0.0)
    faces = one(first_lane) + one(last_lane)
    faces = faces + one((row == ROW0) & (j == 0)) + one((row == ROW0 + ny - 1) & (j == gy - 1))
    x_faces = {3: one(i == 0), 2 + nx: one(i == gx - 1)}

    get_lab.wait()
    get_tab.wait()
    t0, t1, t2 = tab_ref[0], tab_ref[1], tab_ref[2]
    each(0, "wait_recv")

    def conduct(label):
        k = jnp.where(label == 0, t0, jnp.where(label == 1, t1, t2))
        return jnp.where(label < 0, TINY, k)

    nk = nx + 6
    k = [conduct(L[x]) for x in range(nk)]

    hx = [harmonic(k[x], k[x + 1]) for x in range(nk - 1)]
    hy, hz, edge, diag, inv = ([None] * nk for _ in range(5))
    for x in range(1, nk - 1):
        a = k[x]
        hy[x] = harmonic(a, shift(a, -1, 0))
        hz[x] = harmonic(a, jnp.where(last_lane, 0.0, shift(a, -1, 1)))
        edge[x] = a * ((faces + x_faces[x]) if x in x_faces else faces)
        diag[x] = (hx[x - 1] + hx[x]) + (hy[x] + shift(hy[x], 1, 0)) + (hz[x] + shift(hz[x], 1, 1)) + edge[x]
        inv[x] = OMEGA * inverse(jnp.maximum(diag[x], TINY))

    nm = mx + 4
    gxu = [None] * nm
    gyu, gzu, medge, mdiag, minv = ([None] * nm for _ in range(5))

    def middle(m):
        x = 2 * m - 1
        for t in (m - 1, m):
            if gxu[t] is None:
                gxu[t] = pair(pair(hx[2 * t], 0), 1)
        gyu[m] = upper(pair(hy[x] + hy[x + 1], 1), 0)
        gzu[m] = upper(pair(hz[x] + hz[x + 1], 0), 1)
        medge[m] = pair(pair(edge[x] + edge[x + 1], 0), 1)
        mdiag[m] = (gxu[m - 1] + gxu[m]) + (gyu[m] + shift(gyu[m], 2, 0))
        mdiag[m] = mdiag[m] + (gzu[m] + shift(gzu[m], 2, 1)) + medge[m]
        minv[m] = OMEGA * inverse(jnp.maximum(mdiag[m], TINY))

    for m in range(2, nm - 2):
        middle(m)

    get_rhs.wait()
    each(1, "wait_recv")
    u1, u2 = [None] * nk, [None] * nk
    for x in range(1, nk - 1):
        u1[x] = R[x - 1] * inv[x]
    for x in range(2, nk - 2):
        around = flow(hx[x - 1], hx[x], hy[x], hz[x], u1[x - 1], u1[x], u1[x + 1], 1)
        u2[x] = (1.0 + KEEP) * u1[x] + inv[x] * around
    res = [None] * nk
    for x in range(3, nk - 3):
        around = flow(hx[x - 1], hx[x], hy[x], hz[x], u2[x - 1], u2[x], u2[x + 1], 1)
        res[x] = diag[x] * (u1[x] * (1.0 / OMEGA) - u2[x]) + around

    for m in range(2, nm - 2):
        x = 2 * m - 1
        source = pair(pair(res[x] + res[x + 1], 0), 1)
        V1[m, rows, :] = (source * minv[m])[rows]
    each(2, "start")
    for m in (1, nm - 2):
        middle(m)

    def cells(v):
        return jnp.concatenate([v[0:1] + v[2:3], v[4:5] + v[6:7]], axis=0)

    m = 2
    uz = jnp.where((lane & 2) == 2, gzu[m] + gzu[m + 1], 0.0)
    parts = (gxu[m + 1], gyu[m] + gyu[m + 1], uz, medge[m] + medge[m + 1])
    got = exact_dot(jnp.concatenate([p[rows] for p in parts], axis=0), to_cell[...])
    ux, uy, uz, ue = (got[p * ny:(p + 1) * ny] for p in range(4))
    own_cc[0] = cells(ux)
    own_cc[1] = jnp.concatenate([uy[2:3], uy[6:7]], axis=0)
    own_cc[2] = cells(uz)
    own_cc[3] = cells(ue)

    along_gy = [(i, lax.rem(j + b, gy)) for b in range(1, gy)]
    along_gx = [(lax.rem(i + a, gx), j) for a in range(1, gx)]
    spot_cc = CC.at[:, i, pl.ds(2 * j, 2), :]
    line_cc = CC.at[:, i]

    def to_each(devices, src, dst, which):
        for dev in devices:
            pltpu.make_async_remote_copy(
                src_ref=src, dst_ref=dst, send_sem=g_send.at[which], recv_sem=g_recv.at[which],
                device_id=dev, device_id_type=MESH,
            ).start()

    to_each(along_gy, own_cc, spot_cc, 0)
    pltpu.make_async_copy(own_cc, spot_cc, g_recv.at[0]).start()

    spot_cb = CB.at[i, pl.ds(2 * j, 2), :]

    each(2, "wait_recv")
    v1 = [V1[m] for m in range(nm)]
    v2 = [None] * nm
    for m in range(1, nm - 1):
        around = flow(gxu[m - 1], gxu[m], gyu[m], gzu[m], v1[m - 1], v1[m], v1[m + 1], 2)
        v2[m] = (1.0 + KEEP) * v1[m] + minv[m] * around
    for m in range(2, nm - 2):
        V2[m, rows, :] = v2[m][rows]
    pltpu.make_async_copy(line_cc, line_cc, g_recv.at[0]).wait()
    to_each(along_gx, line_cc, line_cc, 1)
    total = None
    for m in range(2, nm - 2):
        around = flow(gxu[m - 1], gxu[m], gyu[m], gzu[m], v2[m - 1], v2[m], v2[m + 1], 2)
        r = mdiag[m] * (v1[m] * (1.0 / OMEGA) - v2[m]) + around
        total = r if total is None else total + r
    own_cb[...] = cells(exact_dot(total[rows], to_cell[...]))
    for_others(lambda dev: pltpu.make_async_remote_copy(
        src_ref=own_cb, dst_ref=spot_cb, send_sem=g_send.at[2], recv_sem=g_recv.at[2],
        device_id=dev, device_id_type=MESH,
    ).start())
    pltpu.make_async_copy(own_cb, spot_cb, g_recv.at[2]).start()
    each(3, "start")

    pltpu.make_async_copy(bytes_cx, bytes_cx, g_recv.at[1]).wait()
    cx, cy, cz, ce = CC[0], CC[1], CC[2], CC[3]

    def before(v):
        return jnp.concatenate([v[-1:], v[:-1]], axis=0)

    def after(v):
        return jnp.concatenate([v[1:], v[:1]], axis=0)

    cxl = before(cx)
    cdiag = (cx + cxl) + (cy + shift(cy, 1, 1)) + (cz + shift(cz, 1, 2)) + ce
    cinv = OMEGA * inverse(cdiag)
    cyl, czl = shift(cy, 1, 1) * cinv, shift(cz, 1, 2) * cinv
    cx, cxl, cy, cz = cx * cinv, cxl * cinv, cy * cinv, cz * cinv
    pltpu.make_async_copy(CB, CB, g_recv.at[2]).wait()
    b = CB[...] * cinv
    v = b
    for step in range(SWEEPS - 1):
        around = cxl * before(v) + cx * after(v)
        around = around + cyl * shift(v, 1, 1) + cy * shift(v, -1, 1)
        around = around + czl * shift(v, 1, 2) + cz * shift(v, -1, 2)
        v = KEEP * v + b + around
    CR[1:gx + 1, 8:8 + v.shape[1], :] = v

    near = [CR[i + p, pl.ds(7 + 2 * j + c, 1), :] for p in range(3) for c in range(4)]
    near = exact_dot(jnp.concatenate(near + [jnp.zeros((4, nz // 4), jnp.float32)], axis=0), to_lane[...])
    near = [
        jnp.concatenate([jnp.broadcast_to(near[4 * p + c:4 * p + c + 1], (4, nz)) for c in range(4)], axis=0)
        for p in range(3)
    ]
    each(3, "wait_recv")
    w = [V2[m] + near[m // 2] for m in range(nm)]
    v3 = [None] * nm
    for m in range(1, nm - 1):
        around = flow(gxu[m - 1], gxu[m], gyu[m], gzu[m], w[m - 1], w[m], w[m + 1], 2)
        v3[m] = KEEP * w[m] + v1[m] + minv[m] * around
    f = [None] * nk
    for x in range(2, nk - 2):
        f[x] = u2[x] + v3[(x + 1) // 2]
    for x in range(3, nk - 3):
        around = flow(hx[x - 1], hx[x], hy[x], hz[x], f[x - 1], f[x], f[x + 1], 1)
        out_ref[x - 3] = (KEEP * f[x] + u1[x] + inv[x] * around)[rows]

    for which in range(4):
        each(which, "wait_send")
    for which, amount in enumerate((bytes_cy, bytes_cx, bytes_cb)):
        pltpu.make_async_copy(amount, amount, g_send.at[which]).wait()


def shards(gx, gy, right_side, labels, conduct_table):
    nx, ny, nz = right_side.shape
    n = gx * gy
    deep = 2 * ROW0 + ny
    cy, cz = gy * (ny // 4), nz // 4
    f32 = jnp.float32
    return pl.pallas_call(
        functools.partial(kernel, gx, gy, nx, ny),
        out_shape=jax.ShapeDtypeStruct(right_side.shape, f32),
        in_specs=[
            pl.BlockSpec(memory_space=pltpu.HBM),
            pl.BlockSpec(memory_space=pltpu.HBM),
            pl.BlockSpec(memory_space=pltpu.HBM),
        ],
        out_specs=pl.BlockSpec(memory_space=pltpu.VMEM),
        scratch_shapes=[
            pltpu.VMEM((nx + 6, deep, nz), jnp.int32),
            pltpu.VMEM((nx + 4, deep, nz), f32),
            pltpu.VMEM((nx // 2 + 4, deep, nz), f32),
            pltpu.VMEM((nx // 2 + 4, deep, nz), f32),
            pltpu.VMEM((4, gx, cy, cz), f32),
            pltpu.VMEM((gx, cy, cz), f32),
            pltpu.VMEM((gx + 2, cy + 16, cz), f32),
            pltpu.VMEM((4, 2, cz), f32),
            pltpu.VMEM((2, cz), f32),
            pltpu.VMEM((gy - 1, 4, 2, cz), f32),
            pltpu.VMEM((gx - 1, 4, cy, cz), f32),
            pltpu.VMEM((n - 1, 2, cz), f32),
            pltpu.SMEM((3,), f32),
            pltpu.VMEM((nz, cz), jnp.bfloat16),
            pltpu.VMEM((cz, nz), jnp.bfloat16),
            pltpu.SemaphoreType.DMA((4, 8)),
            pltpu.SemaphoreType.DMA((4, 8)),
            pltpu.SemaphoreType.DMA((3,)),
            pltpu.SemaphoreType.DMA((3,)),
            pltpu.SemaphoreType.DMA((3,)),
        ],
        compiler_params=pltpu.CompilerParams(
            collective_id=0, has_side_effects=True, vmem_limit_bytes=48 * 1024 * 1024
        ),
    )(*(pltpu.with_memory_space_constraint(x, pltpu.HBM) for x in (right_side, labels, conduct_table)))


def solution(mesh):
    in_specs = (P("gx", "gy", None), P("gx", "gy", None), P())
    return jax.shard_map(
        functools.partial(shards, mesh.shape["gx"], mesh.shape["gy"]),
        mesh=mesh,
        in_specs=in_specs,
        out_specs=P("gx", "gy", None),
        check_vma=False,
    )
```

```python
import functools

import jax
import jax.numpy as jnp
from jax import lax
from jax.experimental import pallas as pl
from jax.experimental.pallas import tpu as pltpu
from jax.sharding import PartitionSpec as P

SWEEPS = 8
OMEGA = 0.8
KEEP = 1.0 - OMEGA
MESH = pl.DeviceIdType.MESH
TINY = 1e-30

DIRECTIONS = ((1, 0), (-1, 0), (0, 1), (0, -1), (1, 1), (1, -1), (-1, 1), (-1, -1))

ROW0 = 4


def span(step, width, count, first):
    if step == 0:
        return first, first, count
    if step > 0:
        return first + count - width, first - width, width
    return first, first + count, width


def shift(v, by, axis):
    return pltpu.roll(v, by % v.shape[axis], axis)


def flow(low, high, hy, hz, v_low, v, v_high, s):
    a, b = v.ndim - 2, v.ndim - 1
    total = low * v_low + high * v_high
    total = total + hy * shift(v, -s, a) + shift(hy * v, s, a)
    return total + hz * shift(v, -s, b) + shift(hz * v, s, b)


def turn(v, by, axis):
    tile = 8 if axis == 0 else 128
    parts = [lax.slice_in_dim(v, p, p + tile, axis=axis) for p in range(0, v.shape[axis], tile)]
    return jnp.concatenate([pltpu.roll(p, by % tile, axis) for p in parts], axis=axis)


def inverse(d):
    r = pl.reciprocal(d, approx=True)
    return r * (2.0 - d * r)


def harmonic(a, b):
    return (2.0 * (a * b)) * inverse(a + b)


def exact_dot(a, ones):
    rounded = lambda x: x.astype(jnp.bfloat16).astype(jnp.float32)
    head = rounded(a)
    rest = a - head
    middle = rounded(rest)
    parts = jnp.concatenate([head, middle, rest - middle], axis=0).astype(jnp.bfloat16)
    out = jnp.dot(parts, ones, preferred_element_type=jnp.float32)
    n = a.shape[0]
    return out[:n] + out[n:2 * n] + out[2 * n:]


def kernel(gx, gy, nx, ny, rhs_hbm, lab_hbm, tab_hbm, out_ref, K, R, V1, V2, CC, CB, CR, own_cc, own_cb,
           bytes_cy, bytes_cx, bytes_cb, lab_ref, tab_ref, to_cell, to_lane, send, recv, g_send, g_recv, fetch):
    i = lax.axis_index("gx")
    j = lax.axis_index("gy")
    n = gx * gy
    me = i * gy + j
    nz = lab_ref.shape[2]
    mx = nx // 2
    tile = (2 * ROW0 + ny, nz)
    rows = slice(ROW0, ROW0 + ny)

    get_lab = pltpu.make_async_copy(lab_hbm, lab_ref, fetch.at[0])
    get_tab = pltpu.make_async_copy(tab_hbm, tab_ref, fetch.at[1])
    get_rhs = pltpu.make_async_copy(rhs_hbm, R.at[2:2 + nx, rows, :], fetch.at[2])
    get_lab.start()
    get_tab.start()

    K[...] = jnp.full(K.shape, TINY, jnp.float32)
    for buf in (R, V1, V2):
        buf[...] = jnp.zeros(buf.shape, jnp.float32)

    def for_others(what):
        if n <= 64:
            ti = [i] + [lax.rem(i + a, gx) for a in range(1, gx)]
            tj = [j] + [lax.rem(j + b, gy) for b in range(1, gy)]
            for b in reversed(range(gy)):
                for a in range(gx):
                    if a or b:
                        what((ti[a], tj[b]))
        else:
            def one(k, c):
                t = lax.rem(me + k, n)
                what((lax.div(t, gy), lax.rem(t, gy)))
                return c

            lax.fori_loop(1, n, one, 0)

    barrier = pltpu.get_barrier_semaphore()
    for_others(lambda dev: pl.semaphore_signal(barrier, inc=1, device_id=dev, device_id_type=MESH))
    get_rhs.start()

    get_lab.wait()
    get_tab.wait()
    t0, t1, t2 = tab_ref[0], tab_ref[1], tab_ref[2]
    labels = lab_ref[...]
    K[3:3 + nx, rows, :] = jnp.where(labels == 0, t0, jnp.where(labels == 1, t1, t2))
    pl.semaphore_wait(barrier, n - 1)

    def there(dx, dy):
        ok = None
        for at, d, size in ((i, dx, gx), (j, dy, gy)):
            if d:
                c = (at < size - 1) if d > 0 else (at > 0)
                ok = c if ok is None else jnp.logical_and(ok, c)
        return ok

    def halo_copy(buf, which, d, x0, cx, y0, cy, wx, wy, corner_x, corner_y):
        dx, dy = DIRECTIONS[d]
        both = dx != 0 and dy != 0
        sx, tx, lx = span(dx, corner_x if both else wx, cx, x0)
        sy, ty, ly = span(dy, corner_y if both else wy, cy, y0)
        return pltpu.make_async_remote_copy(
            src_ref=buf.at[sx:sx + lx, sy:sy + ly, :],
            dst_ref=buf.at[tx:tx + lx, ty:ty + ly, :],
            send_sem=send.at[which, d],
            recv_sem=recv.at[which, d],
            device_id=(i + dx, j + dy),
            device_id_type=MESH,
        )

    halos = {
        0: (K, 3, nx, ROW0, ny, 3, 3, 2, 2),
        1: (R, 2, nx, ROW0, ny, 2, 2, 1, 1),
        2: (V1, 2, mx, ROW0, ny, 2, 4, 1, 2),
        3: (V2, 2, mx, ROW0, ny, 2, 4, 1, 2),
    }

    def each(which, what):
        for d, (dx, dy) in enumerate(DIRECTIONS):
            sign = -1 if what == "wait_recv" else 1

            @pl.when(there(sign * dx, sign * dy))
            def _():
                buf, *sizes = halos[which]
                getattr(halo_copy(buf, which, d, *sizes), what)()

    each(0, "start")
    get_rhs.wait()
    each(1, "start")

    z = lax.broadcasted_iota(jnp.int32, (nz, nz // 4), 0)
    q = lax.broadcasted_iota(jnp.int32, (nz, nz // 4), 1)
    to_cell[...] = jnp.where(((z >> 2) == q) & ((z & 1) == 0), 1.0, 0.0).astype(jnp.bfloat16)
    q = lax.broadcasted_iota(jnp.int32, (nz // 4, nz), 0)
    z = lax.broadcasted_iota(jnp.int32, (nz // 4, nz), 1)
    to_lane[...] = jnp.where((z >> 2) == q, 1.0, 0.0).astype(jnp.bfloat16)
    CR[...] = jnp.zeros(CR.shape, jnp.float32)

    row = lax.broadcasted_iota(jnp.int32, tile, 0)
    lane = lax.broadcasted_iota(jnp.int32, tile, 1)
    odd_row = (row & 1) == 1
    odd_lane = (lane & 1) == 1
    last_lane = lane == nz - 1
    first_lane = lane == 0

    def pair(v, axis):
        odd = odd_row if axis == 0 else odd_lane
        return v + jnp.where(odd, turn(v, 1, axis), turn(v, -1, axis))

    def upper(v, axis):
        odd = odd_row if axis == 0 else odd_lane
        return jnp.where(odd, v, turn(v, -1, axis))

    one = lambda c: jnp.where(c, 1.0, 0.0)
    faces = one(first_lane) + one(last_lane)
    faces = faces + one((row == ROW0) & (j == 0)) + one((row == ROW0 + ny - 1) & (j == gy - 1))
    x_faces = {3: one(i == 0), 2 + nx: one(i == gx - 1)}

    each(0, "wait_recv")
    nk = nx + 6
    k = [K[x] for x in range(nk)]

    hx = [harmonic(k[x], k[x + 1]) for x in range(nk - 1)]
    hy, hz, edge, diag, inv = ([None] * nk for _ in range(5))
    for x in range(1, nk - 1):
        a = k[x]
        hy[x] = harmonic(a, shift(a, -1, 0))
        hz[x] = harmonic(a, jnp.where(last_lane, 0.0, shift(a, -1, 1)))
        edge[x] = a * ((faces + x_faces[x]) if x in x_faces else faces)
        diag[x] = (hx[x - 1] + hx[x]) + (hy[x] + shift(hy[x], 1, 0)) + (hz[x] + shift(hz[x], 1, 1)) + edge[x]
        inv[x] = OMEGA * inverse(jnp.maximum(diag[x], TINY))

    nm = mx + 4
    gxu = [None] * nm
    gyu, gzu, medge, mdiag, minv = ([None] * nm for _ in range(5))

    def middle(m):
        x = 2 * m - 1
        for t in (m - 1, m):
            if gxu[t] is None:
                gxu[t] = pair(pair(hx[2 * t], 0), 1)
        gyu[m] = upper(pair(hy[x] + hy[x + 1], 1), 0)
        gzu[m] = upper(pair(hz[x] + hz[x + 1], 0), 1)
        medge[m] = pair(pair(edge[x] + edge[x + 1], 0), 1)
        mdiag[m] = (gxu[m - 1] + gxu[m]) + (gyu[m] + shift(gyu[m], 2, 0))
        mdiag[m] = mdiag[m] + (gzu[m] + shift(gzu[m], 2, 1)) + medge[m]
        minv[m] = OMEGA * inverse(jnp.maximum(mdiag[m], TINY))

    for m in range(2, nm - 2):
        middle(m)

    each(1, "wait_recv")
    u1, u2 = [None] * nk, [None] * nk
    for x in range(1, nk - 1):
        u1[x] = R[x - 1] * inv[x]
    for x in range(2, nk - 2):
        around = flow(hx[x - 1], hx[x], hy[x], hz[x], u1[x - 1], u1[x], u1[x + 1], 1)
        u2[x] = (1.0 + KEEP) * u1[x] + inv[x] * around
    res = [None] * nk
    for x in range(3, nk - 3):
        around = flow(hx[x - 1], hx[x], hy[x], hz[x], u2[x - 1], u2[x], u2[x + 1], 1)
        res[x] = diag[x] * (u1[x] * (1.0 / OMEGA) - u2[x]) + around

    for m in range(2, nm - 2):
        x = 2 * m - 1
        source = pair(pair(res[x] + res[x + 1], 0), 1)
        V1[m, rows, :] = (source * minv[m])[rows]
    each(2, "start")
    for m in (1, nm - 2):
        middle(m)

    def cells(v):
        return jnp.concatenate([v[0:1] + v[2:3], v[4:5] + v[6:7]], axis=0)

    m = 2
    uz = jnp.where((lane & 2) == 2, gzu[m] + gzu[m + 1], 0.0)
    parts = (gxu[m + 1], gyu[m] + gyu[m + 1], uz, medge[m] + medge[m + 1])
    got = exact_dot(jnp.concatenate([p[rows] for p in parts], axis=0), to_cell[...])
    ux, uy, uz, ue = (got[p * ny:(p + 1) * ny] for p in range(4))
    own_cc[0] = cells(ux)
    own_cc[1] = jnp.concatenate([uy[2:3], uy[6:7]], axis=0)
    own_cc[2] = cells(uz)
    own_cc[3] = cells(ue)

    along_gy = [(i, lax.rem(j + b, gy)) for b in range(1, gy)]
    along_gx = [(lax.rem(i + a, gx), j) for a in range(1, gx)]
    spot_cc = CC.at[:, i, pl.ds(2 * j, 2), :]
    line_cc = CC.at[:, i]

    def to_each(devices, src, dst, which):
        for dev in devices:
            pltpu.make_async_remote_copy(
                src_ref=src, dst_ref=dst, send_sem=g_send.at[which], recv_sem=g_recv.at[which],
                device_id=dev, device_id_type=MESH,
            ).start()

    to_each(along_gy, own_cc, spot_cc, 0)
    pltpu.make_async_copy(own_cc, spot_cc, g_recv.at[0]).start()

    spot_cb = CB.at[i, pl.ds(2 * j, 2), :]

    each(2, "wait_recv")
    v1 = [V1[m] for m in range(nm)]
    v2 = [None] * nm
    for m in range(1, nm - 1):
        around = flow(gxu[m - 1], gxu[m], gyu[m], gzu[m], v1[m - 1], v1[m], v1[m + 1], 2)
        v2[m] = (1.0 + KEEP) * v1[m] + minv[m] * around
    for m in range(2, nm - 2):
        V2[m, rows, :] = v2[m][rows]
    pltpu.make_async_copy(line_cc, line_cc, g_recv.at[0]).wait()
    to_each(along_gx, line_cc, line_cc, 1)
    total = None
    for m in range(2, nm - 2):
        around = flow(gxu[m - 1], gxu[m], gyu[m], gzu[m], v2[m - 1], v2[m], v2[m + 1], 2)
        r = mdiag[m] * (v1[m] * (1.0 / OMEGA) - v2[m]) + around
        total = r if total is None else total + r
    own_cb[...] = cells(exact_dot(total[rows], to_cell[...]))
    for_others(lambda dev: pltpu.make_async_remote_copy(
        src_ref=own_cb, dst_ref=spot_cb, send_sem=g_send.at[2], recv_sem=g_recv.at[2],
        device_id=dev, device_id_type=MESH,
    ).start())
    pltpu.make_async_copy(own_cb, spot_cb, g_recv.at[2]).start()
    each(3, "start")

    pltpu.make_async_copy(bytes_cx, bytes_cx, g_recv.at[1]).wait()
    cx, cy, cz, ce = CC[0], CC[1], CC[2], CC[3]

    def before(v):
        return jnp.concatenate([v[-1:], v[:-1]], axis=0)

    def after(v):
        return jnp.concatenate([v[1:], v[:1]], axis=0)

    cxl = before(cx)
    cdiag = (cx + cxl) + (cy + shift(cy, 1, 1)) + (cz + shift(cz, 1, 2)) + ce
    cinv = OMEGA * inverse(cdiag)
    cyl, czl = shift(cy, 1, 1) * cinv, shift(cz, 1, 2) * cinv
    cx, cxl, cy, cz = cx * cinv, cxl * cinv, cy * cinv, cz * cinv
    pltpu.make_async_copy(CB, CB, g_recv.at[2]).wait()
    b = CB[...] * cinv
    v = b
    for step in range(SWEEPS - 1):
        around = cxl * before(v) + cx * after(v)
        around = around + cyl * shift(v, 1, 1) + cy * shift(v, -1, 1)
        around = around + czl * shift(v, 1, 2) + cz * shift(v, -1, 2)
        v = KEEP * v + b + around
    CR[1:gx + 1, 8:8 + v.shape[1], :] = v

    near = [CR[i + p, pl.ds(7 + 2 * j + c, 1), :] for p in range(3) for c in range(4)]
    near = exact_dot(jnp.concatenate(near + [jnp.zeros((4, nz // 4), jnp.float32)], axis=0), to_lane[...])
    near = [
        jnp.concatenate([jnp.broadcast_to(near[4 * p + c:4 * p + c + 1], (4, nz)) for c in range(4)], axis=0)
        for p in range(3)
    ]
    each(3, "wait_recv")
    w = [V2[m] + near[m // 2] for m in range(nm)]
    v3 = [None] * nm
    for m in range(1, nm - 1):
        around = flow(gxu[m - 1], gxu[m], gyu[m], gzu[m], w[m - 1], w[m], w[m + 1], 2)
        v3[m] = KEEP * w[m] + v1[m] + minv[m] * around
    f = [None] * nk
    for x in range(2, nk - 2):
        f[x] = u2[x] + v3[(x + 1) // 2]
    for x in range(3, nk - 3):
        around = flow(hx[x - 1], hx[x], hy[x], hz[x], f[x - 1], f[x], f[x + 1], 1)
        out_ref[x - 3] = (KEEP * f[x] + u1[x] + inv[x] * around)[rows]

    for which in range(4):
        each(which, "wait_send")
    for which, amount in enumerate((bytes_cy, bytes_cx, bytes_cb)):
        pltpu.make_async_copy(amount, amount, g_send.at[which]).wait()


def shards(gx, gy, right_side, labels, conduct_table):
    nx, ny, nz = right_side.shape
    n = gx * gy
    deep = 2 * ROW0 + ny
    cy, cz = gy * (ny // 4), nz // 4
    f32 = jnp.float32
    return pl.pallas_call(
        functools.partial(kernel, gx, gy, nx, ny),
        out_shape=jax.ShapeDtypeStruct(right_side.shape, f32),
        in_specs=[
            pl.BlockSpec(memory_space=pltpu.HBM),
            pl.BlockSpec(memory_space=pltpu.HBM),
            pl.BlockSpec(memory_space=pltpu.HBM),
        ],
        out_specs=pl.BlockSpec(memory_space=pltpu.VMEM),
        scratch_shapes=[
            pltpu.VMEM((nx + 6, deep, nz), f32),
            pltpu.VMEM((nx + 4, deep, nz), f32),
            pltpu.VMEM((nx // 2 + 4, deep, nz), f32),
            pltpu.VMEM((nx // 2 + 4, deep, nz), f32),
            pltpu.VMEM((4, gx, cy, cz), f32),
            pltpu.VMEM((gx, cy, cz), f32),
            pltpu.VMEM((gx + 2, cy + 16, cz), f32),
            pltpu.VMEM((4, 2, cz), f32),
            pltpu.VMEM((2, cz), f32),
            pltpu.VMEM((gy - 1, 4, 2, cz), f32),
            pltpu.VMEM((gx - 1, 4, cy, cz), f32),
            pltpu.VMEM((n - 1, 2, cz), f32),
            pltpu.VMEM((nx, ny, nz), jnp.int32),
            pltpu.SMEM((3,), f32),
            pltpu.VMEM((nz, cz), jnp.bfloat16),
            pltpu.VMEM((cz, nz), jnp.bfloat16),
            pltpu.SemaphoreType.DMA((4, 8)),
            pltpu.SemaphoreType.DMA((4, 8)),
            pltpu.SemaphoreType.DMA((3,)),
            pltpu.SemaphoreType.DMA((3,)),
            pltpu.SemaphoreType.DMA((3,)),
        ],
        compiler_params=pltpu.CompilerParams(
            collective_id=0, has_side_effects=True, vmem_limit_bytes=48 * 1024 * 1024
        ),
    )(*(pltpu.with_memory_space_constraint(x, pltpu.HBM) for x in (right_side, labels, conduct_table)))


def solution(mesh):
    in_specs = (P("gx", "gy", None), P("gx", "gy", None), P())
    return jax.shard_map(
        functools.partial(shards, mesh.shape["gx"], mesh.shape["gy"]),
        mesh=mesh,
        in_specs=in_specs,
        out_specs=P("gx", "gy", None),
        check_vma=False,
    )
```
